128 devices in a mesh: marker: 4 (over z_hi, core), animal: 32 (over x, y, z_lo).
Axes of the slice: x: 4, y: 4, z: 4 (z_hi: 2, z_lo: 2; z = z_hi * 2 + z_lo), core: 2. Of those that a mesh axis runs over, the one named last changes fastest.
Arguments:
- genotypes: int32 [24576, 32768], P('animal', 'marker'), may hold values from 0 to 2
- frequencies: bfloat16 [32768, 512], P('marker'), may hold values from -0.0625 to 0.0625
- phases: float32 [512], replicated, may hold values from -3.140625 to 3.140625
- phenotypes: bfloat16 [24576, 64], P('animal'), may hold values from -6 to 6
Outputs:
- gram: float32 [512, 512], P('animal')
- cross: float32 [512, 64], P('animal')
The draws below stay inside these ranges and needn't reach their ends.
All inputs are finite; a program needn't handle non-finite values.
Results may differ from the reference program's by a relative error of at most 0.0029.
Values may be sent and summed in bfloat16 or wider, within the bound.
No kernel may reach another device: no remote copies, remote signals or barrier semaphores. Data moves between devices by JAX's collectives and lax.ppermute only.
A program may use at most 128 MiB of HBM per device.

```python
import math
import jax
import jax.numpy as jnp
from jax import lax

MARKERS = 32768
FEATS = 512
TRAITS = 64
TOKENS = 24576


def touch_ends(result, stream_key, smallest, top_value):
    longest = result.shape.index(max(result.shape))
    spots = []
    for shift in (0, 1):
        where = [jax.random.randint(jax.random.fold_in(stream_key, axis), (), 0, length) for axis, length in enumerate(result.shape)]
        where[longest] = (where[longest] + shift) % result.shape[longest]
        spots.append(tuple(where))
    return result.at[spots[0]].set(smallest).at[spots[1]].set(top_value)


def steps_of(key, extent, pieces, least, largest):
    loudness, own = 1.0, jax.random.fold_in(key, 6)
    for position, blocks in pieces:
        heights = jnp.exp(jax.random.uniform(jax.random.fold_in(own, position), (blocks,), jnp.float32, least / len(pieces), largest / len(pieces)))
        loudness = loudness * jnp.repeat(heights, extent[position] // blocks).reshape([-1 if axis == position else 1 for axis in range(len(extent))])
    return loudness


def bell_draw(key, dims, deviation, bound, pieces=(), kind=jnp.bfloat16):
    array = deviation * jax.random.normal(key, dims, jnp.float32)
    if pieces:
        array = array * steps_of(key, dims, pieces, -0.22, 0.18)
    return jnp.clip(array, -bound, bound).astype(kind)


def setup_inputs(seed: int = 0) -> dict:
    seeds = jax.random.split(jax.random.key(seed), 5)
    return {
        "genotypes": touch_ends(jax.random.randint(seeds[0], (TOKENS, MARKERS), 0, 3), jax.random.fold_in(seeds[0], 1), 0, 2).astype(jnp.int32),
        "frequencies": bell_draw(seeds[1], (MARKERS, FEATS), (MARKERS // 4) ** -0.5, 0.0625, ((0, 4),)),
        "phases": jnp.clip(jax.random.uniform(seeds[2], (FEATS,), jnp.float32, -3.140625, 3.140625), -3.140625, 3.140625),
        "phenotypes": bell_draw(seeds[3], (TOKENS, TRAITS), 1.0, 6.0, ((0, 32),)),
    }


def reference(genotypes, frequencies, phases, phenotypes):
    block_rows = min(TOKENS, 512)
    block_count = TOKENS // block_rows
    geno_blocks = genotypes.reshape(block_count, block_rows, MARKERS)
    phen_blocks = phenotypes.reshape(block_count, block_rows, TRAITS)
    panel = frequencies.astype(jnp.float32)

    def accumulate(running, blocks):
        geno_block, phen_block = blocks
        dosage = (geno_block - 1).astype(jnp.float32)
        projection = jnp.dot(dosage, panel, precision=lax.Precision.HIGHEST, preferred_element_type=jnp.float32)
        features = (math.sqrt(2.0) * jnp.cos(projection + phases)).astype(jnp.bfloat16)
        widened = features.astype(jnp.float32)
        gram_sum = running[0] + jnp.dot(widened.T, widened, precision=lax.Precision.HIGHEST)
        cross_sum = running[1] + jnp.dot(widened.T, phen_block.astype(jnp.float32), precision=lax.Precision.HIGHEST)
        return ((gram_sum, cross_sum), None)
    start_sums = (jnp.zeros((FEATS, FEATS), jnp.float32), jnp.zeros((FEATS, TRAITS), jnp.float32))
    sums, unused = lax.scan(accumulate, start_sums, (geno_blocks, phen_blocks))
    return (sums[0] / TOKENS, sums[1] / math.sqrt(TOKENS))
```

```python
import functools
import math

import jax
import jax.numpy as jnp
from jax import lax
from jax.experimental import pallas as pl
from jax.experimental.pallas import tpu as pltpu
from jax.sharding import PartitionSpec as P

OTHER_CORE = [(0, 1), (1, 0), (2, 3), (3, 2)]
OTHER_CHIP = [(0, 2), (2, 0), (1, 3), (3, 1)]
STEP = 1024
SINE = (-8.88576566829991, 58.46592923637672, -115.4012466635561, 108.25774031408996, -55.913345915340486)


def to_turns(radians):
    steps = jnp.round(radians * (65536.0 / (2.0 * math.pi))).astype(jnp.int32)
    return ((steps << 16) >> 16).astype(jnp.int16)


def accumulate(geno, panel, acc):
    dosage = (geno - 1).astype(jnp.float32).astype(jnp.bfloat16)
    acc[...] += jnp.dot(dosage, panel, preferred_element_type=jnp.float32)


def first_half_kernel(geno_hbm, panel_hbm, out_ref, panel_ref, geno_buf, acc, geno_sem, panel_sem):
    rows = acc.shape[0]
    steps = geno_buf.shape[0]
    first = pl.multiple_of((1 - lax.axis_index("marker") % 2) * rows, rows)

    def panel_copy(k):
        part = pl.ds(pl.multiple_of(k * STEP, STEP), STEP)
        return pltpu.make_async_copy(panel_hbm.at[part], panel_ref.at[part], panel_sem.at[k])

    def geno_copy(k):
        part = pl.ds(pl.multiple_of(k * STEP, STEP), STEP)
        return pltpu.make_async_copy(geno_hbm.at[pl.ds(first, rows), part], geno_buf.at[k], geno_sem.at[k])

    for k in range(steps):
        panel_copy(k).start()
        geno_copy(k).start()
    acc[...] = jnp.zeros_like(acc)

    @pl.loop(0, steps)
    def _(k):
        panel_copy(k).wait()
        geno_copy(k).wait()
        accumulate(geno_buf[k], panel_ref[pl.ds(pl.multiple_of(k * STEP, STEP), STEP)], acc)

    out_ref[...] = to_turns(acc[...])


def second_half_kernel(geno_hbm, panel_ref, out_ref, geno_buf, acc, geno_sem):
    rows = acc.shape[0]
    steps = geno_buf.shape[0]
    first = pl.multiple_of((lax.axis_index("marker") % 2) * rows, rows)

    def geno_copy(k):
        part = pl.ds(pl.multiple_of(k * STEP, STEP), STEP)
        return pltpu.make_async_copy(geno_hbm.at[pl.ds(first, rows), part], geno_buf.at[k], geno_sem.at[k])

    for k in range(steps):
        geno_copy(k).start()
    acc[...] = jnp.zeros_like(acc)

    @pl.loop(0, steps)
    def _(k):
        geno_copy(k).wait()
        accumulate(geno_buf[k], panel_ref[pl.ds(pl.multiple_of(k * STEP, STEP), STEP)], acc)

    out_ref[...] = to_turns(acc[...])


def features_kernel(here_ref, there_ref, phase_ref, out_ref):
    turns = here_ref[...].astype(jnp.int32) + there_ref[...].astype(jnp.int32)
    turns = ((turns << 16) >> 16).astype(jnp.float32) * (1.0 / 65536.0)
    turns = turns + phase_ref[...] * (1.0 / (2.0 * math.pi))
    turns = turns - jnp.round(turns)
    t = jnp.abs(turns) - 0.25
    square = t * t
    value = jnp.full_like(t, SINE[-1])
    for factor in SINE[-2::-1]:
        value = value * square + factor
    out_ref[...] = (value * t).astype(jnp.bfloat16)


def gram_kernel(own_ref, other_ref, pheno_ref, out_ref):
    rows, feats = own_ref.shape
    half = feats // 2
    core = lax.axis_index("marker") % 2
    cols = pl.ds(pl.multiple_of(core * half, half), half)
    contract = (((0,), (0,)), ((), ()))

    def product(left, right):
        return lax.dot_general(left, right, contract, preferred_element_type=jnp.float32)

    own_pheno = pheno_ref[pl.ds(pl.multiple_of(core * rows, rows), rows)]
    other_pheno = pheno_ref[pl.ds(pl.multiple_of((1 - core) * rows, rows), rows)]
    gram = product(own_ref[...], own_ref[:, cols]) + product(other_ref[...], other_ref[:, cols])
    cross = product(own_ref[...], own_pheno) + product(other_ref[...], other_pheno)
    high = cross.astype(jnp.bfloat16)
    low = (cross - high.astype(jnp.float32)).astype(jnp.bfloat16)
    out_ref[:, :half] = gram.astype(jnp.bfloat16)
    out_ref[:, half:] = jnp.where(core == 0, high, low)


def sum_kernel(parts, in_ref, out_ref):
    wide = in_ref[...].astype(jnp.float32)
    out_ref[...] = jnp.sum(wide.reshape(parts, wide.shape[0] // parts, wide.shape[1]), axis=0)


def finish_kernel(animals_all, own_ref, other_ref, gram_ref, cross_ref):
    half = gram_ref.shape[1] // 2
    core = lax.axis_index("marker") % 2
    here = pl.ds(pl.multiple_of(core * half, half), half)
    there = pl.ds(pl.multiple_of((1 - core) * half, half), half)
    gram_ref[:, here] = own_ref[:, :half] / animals_all
    gram_ref[:, there] = other_ref[:, :half] / animals_all
    cross_ref[...] = (own_ref[:, half:] + other_ref[:, half:]) / math.sqrt(animals_all)


def vmem():
    return pl.BlockSpec(memory_space=pltpu.VMEM)


def anywhere():
    return pl.BlockSpec(memory_space=pl.ANY)


def on_device(genotypes, frequencies, phases, phenotypes):
    rows, markers = genotypes.shape
    feats = frequencies.shape[1]
    traits = phenotypes.shape[1]
    groups = lax.axis_size("animal")
    animals_all = float(groups * rows)
    half = rows // 2
    steps = markers // STEP
    scratch = [
        pltpu.VMEM((steps, half, STEP), jnp.int32),
        pltpu.VMEM((half, feats), jnp.float32),
        pltpu.SemaphoreType.DMA((steps,)),
    ]
    flops = 2 * half * markers * feats
    params = pltpu.CompilerParams(vmem_limit_bytes=24 * 2**20)
    small = pltpu.CompilerParams(vmem_limit_bytes=12 * 2**20)

    with jax.named_scope("projection_other_rows"):
        to_send, panel = pl.pallas_call(
            first_half_kernel,
            out_shape=(jax.ShapeDtypeStruct((half, feats), jnp.int16), pltpu.VMEM((markers, feats), jnp.bfloat16)),
            in_specs=[anywhere(), anywhere()],
            out_specs=(vmem(), vmem()),
            scratch_shapes=scratch + [pltpu.SemaphoreType.DMA((steps,))],
            compiler_params=params,
            cost_estimate=pl.CostEstimate(flops=flops, bytes_accessed=half * markers * 4 + markers * feats * 2, transcendentals=0),
        )(genotypes, frequencies)
    received = lax.ppermute(to_send, "marker", OTHER_CORE)
    with jax.named_scope("projection_own_rows"):
        kept = pl.pallas_call(
            second_half_kernel,
            out_shape=jax.ShapeDtypeStruct((half, feats), jnp.int16),
            in_specs=[anywhere(), vmem()],
            out_specs=vmem(),
            scratch_shapes=scratch,
            compiler_params=params,
            cost_estimate=pl.CostEstimate(flops=flops, bytes_accessed=half * markers * 4, transcendentals=0),
        )(genotypes, panel)
    chip_sum = kept + received
    chip_other = lax.ppermute(chip_sum, "marker", OTHER_CHIP)
    with jax.named_scope("features"):
        features = pl.pallas_call(
            features_kernel,
            out_shape=jax.ShapeDtypeStruct((half, feats), jnp.bfloat16),
            in_specs=[vmem()] * 3,
            out_specs=vmem(),
            compiler_params=small,
        )(chip_sum, chip_other, phases.reshape(1, feats))
    features_other = lax.ppermute(features, "marker", OTHER_CORE)
    with jax.named_scope("gram_cross"):
        partial_sums = pl.pallas_call(
            gram_kernel,
            out_shape=jax.ShapeDtypeStruct((feats, feats // 2 + traits), jnp.bfloat16),
            in_specs=[vmem()] * 3,
            out_specs=vmem(),
            compiler_params=small,
        )(features, features_other, phenotypes)
    pieces = lax.all_to_all(partial_sums, "animal", 0, 0, tiled=True)
    with jax.named_scope("sum_animals"):
        own = pl.pallas_call(
            functools.partial(sum_kernel, groups),
            out_shape=jax.ShapeDtypeStruct((feats // groups, feats // 2 + traits), jnp.float32),
            in_specs=[vmem()],
            out_specs=vmem(),
            compiler_params=small,
        )(pieces)
    other = lax.ppermute(own, "marker", OTHER_CORE)
    with jax.named_scope("finish"):
        return pl.pallas_call(
            functools.partial(finish_kernel, animals_all),
            out_shape=(
                jax.ShapeDtypeStruct((feats // groups, feats), jnp.float32),
                jax.ShapeDtypeStruct((feats // groups, traits), jnp.float32),
            ),
            in_specs=[vmem()] * 2,
            out_specs=(vmem(), vmem()),
            compiler_params=small,
        )(own, other)


def solution(mesh):
    in_specs = (P("animal", "marker"), P("marker", None), P(), P("animal", None))
    out_specs = (P("animal", None), P("animal", None))
    return jax.shard_map(
        on_device, mesh=mesh, in_specs=in_specs, out_specs=out_specs, check_vma=False
    )
```

```python
import functools
import math

import jax
import jax.numpy as jnp
from jax import lax
from jax.experimental import pallas as pl
from jax.experimental.pallas import tpu as pltpu
from jax.sharding import PartitionSpec as P

OTHER_CORE = [(0, 1), (1, 0), (2, 3), (3, 2)]
OTHER_CHIP = [(0, 2), (2, 0), (1, 3), (3, 1)]
OTHER_BOTH = [(0, 3), (3, 0), (1, 2), (2, 1)]
TILE = 256
PARTS = [(0, 512)] + [(512 + 1024 * k, 1024) for k in range(7)] + [(7680, 512)]
SINE = (-8.88576566829991, 58.46592923637672, -115.4012466635561, 108.25774031408996, -55.913345915340486)


def to_turns(radians):
    steps = jnp.round(radians * (65536.0 / (2.0 * math.pi))).astype(jnp.int32)
    return ((steps << 16) >> 16).astype(jnp.int16)


def project(geno, panel, before, put):
    def run(*sums):
        for step, (start, width) in enumerate(PARTS):
            before(step)
            for tile in range(start, start + width, TILE):
                dosage = (geno[:, tile : tile + TILE] - 1).astype(jnp.float32).astype(jnp.bfloat16)
                slot = tile // TILE % 2
                for unit in range(2):
                    pltpu.matmul_push_rhs(panel[tile : tile + TILE, unit * TILE : (unit + 1) * TILE], slot, unit)
                for unit in range(2):
                    pltpu.matmul_acc_lhs(sums[unit], dosage, slot)
        for unit in range(2):
            put(to_turns(pltpu.matmul_pop(sums[unit])), slice(unit * TILE, (unit + 1) * TILE))

    pl.run_scoped(run, *[pltpu.ACC(unit)((geno.shape[0], TILE), jnp.float32) for unit in range(2)])


def copies(geno_hbm, group, geno, sem):
    rows = geno.shape[0] // 2
    core = lax.axis_index("marker") % 2
    firsts = (pl.multiple_of((group * 2 + 1 - core) * rows, rows), pl.multiple_of((group * 2 + core) * rows, rows))
    return [
        [
            pltpu.make_async_copy(
                geno_hbm.at[pl.ds(first, rows), pl.ds(start, width)],
                geno.at[pl.ds(place * rows, rows), pl.ds(start, width)],
                sem.at[step, place],
            )
            for place, first in enumerate(firsts)
        ]
        for step, (start, width) in enumerate(PARTS)
    ]


def store(send_ref, keep_ref):
    rows = send_ref.shape[0]

    def put(turns, cols):
        send_ref[:, cols] = turns[:rows]
        keep_ref[:, cols] = turns[rows:]

    return put


def first_kernel(geno_hbm, panel_hbm, send_ref, keep_ref, panel_ref, geno, geno_sem, panel_sem):
    chip = lax.axis_index("marker") // 2
    geno_copies = copies(geno_hbm, 1 - chip, geno, geno_sem)
    panel_copies = [
        pltpu.make_async_copy(panel_hbm.at[pl.ds(start, width)], panel_ref.at[pl.ds(start, width)], panel_sem.at[step])
        for step, (start, width) in enumerate(PARTS)
    ]
    for panel_copy, pair in zip(panel_copies, geno_copies):
        for copy in [panel_copy] + pair:
            copy.start()

    def before(step):
        for copy in [panel_copies[step]] + geno_copies[step]:
            copy.wait()

    project(geno, panel_ref, before, store(send_ref, keep_ref))


def second_kernel(geno_hbm, panel_ref, _, send_ref, keep_ref, geno, geno_sem):
    geno_copies = copies(geno_hbm, lax.axis_index("marker") // 2, geno, geno_sem)
    for pair in geno_copies:
        for copy in pair:
            copy.start()

    def before(step):
        for copy in geno_copies[step]:
            copy.wait()

    project(geno, panel_ref, before, store(send_ref, keep_ref))


def features_kernel(kept_ref, core_ref, phase_ref, out_ref):
    turns = kept_ref[...].astype(jnp.int32) + core_ref[...].astype(jnp.int32)
    turns = ((turns << 16) >> 16).astype(jnp.float32) * (1.0 / 65536.0)
    turns = turns + phase_ref[...] * (1.0 / (2.0 * math.pi))
    turns = turns - jnp.round(turns)
    t = jnp.abs(turns) - 0.25
    square = t * t
    value = jnp.full_like(t, SINE[-1])
    for factor in SINE[-2::-1]:
        value = value * square + factor
    out_ref[...] = (value * t).astype(jnp.bfloat16)


def gram_kernel(own_ref, other_ref, pheno_ref, out_ref):
    rows, feats = own_ref.shape
    half = feats // 2
    place = lax.axis_index("marker")
    core = place % 2
    cols = pl.ds(pl.multiple_of(core * half, half), half)
    blocks = [(own_ref, place), (other_ref, place + 1 - 2 * core)]

    def product(left, right):
        return lax.dot_general(left, right, (((0,), (0,)), ((), ())), preferred_element_type=jnp.float32)

    gram = sum(product(ref[...], ref[:, cols]) for ref, _ in blocks)
    cross = sum(product(ref[...], pheno_ref[pl.ds(pl.multiple_of(spot * rows, rows), rows)]) for ref, spot in blocks)
    high = cross.astype(jnp.bfloat16)
    low = (cross - high.astype(jnp.float32)).astype(jnp.bfloat16)
    out_ref[:, :half] = gram.astype(jnp.bfloat16)
    out_ref[:, half:] = jnp.where(core == 0, high, low)


def sum_kernel(parts, in_ref, out_ref):
    wide = in_ref[...].astype(jnp.float32)
    out_ref[...] = jnp.sum(wide.reshape(parts, wide.shape[0] // parts, wide.shape[1]), axis=0)


def finish_kernel(animals_all, own_ref, core_ref, chip_ref, both_ref, gram_ref, cross_ref):
    half = gram_ref.shape[1] // 2
    core = lax.axis_index("marker") % 2
    here = pl.ds(pl.multiple_of(core * half, half), half)
    there = pl.ds(pl.multiple_of((1 - core) * half, half), half)
    own = own_ref[...] + chip_ref[...]
    other = core_ref[...] + both_ref[...]
    gram_ref[:, here] = own[:, :half] / animals_all
    gram_ref[:, there] = other[:, :half] / animals_all
    cross_ref[...] = (own[:, half:] + other[:, half:]) / math.sqrt(animals_all)


def vmem():
    return pl.BlockSpec(memory_space=pltpu.VMEM)


def anywhere():
    return pl.BlockSpec(memory_space=pl.ANY)


def on_device(genotypes, frequencies, phases, phenotypes):
    rows, markers = genotypes.shape
    feats = frequencies.shape[1]
    traits = phenotypes.shape[1]
    groups = lax.axis_size("animal")
    animals_all = float(groups * rows)
    half, quarter = rows // 2, rows // 4
    small = pltpu.CompilerParams(vmem_limit_bytes=12 * 2**20)
    dma = pltpu.SemaphoreType.DMA
    genotypes = pltpu.with_memory_space_constraint(genotypes, pltpu.HBM)
    frequencies = pltpu.with_memory_space_constraint(frequencies, pltpu.HBM)

    def cost(height, more=0):
        return pl.CostEstimate(flops=2 * height * markers * feats, bytes_accessed=height * markers * 4 + more, transcendentals=0)

    part = jax.ShapeDtypeStruct((quarter, feats), jnp.int16)
    geno_scratch = [pltpu.VMEM((half, markers), jnp.int32), dma((len(PARTS), 2))]
    params = pltpu.CompilerParams(vmem_limit_bytes=20 * 2**20)
    with jax.named_scope("projection_other_chip"):
        to_core, kept, panel = pl.pallas_call(
            first_kernel,
            out_shape=(part, part, pltpu.VMEM((markers, feats), jnp.bfloat16)),
            in_specs=[anywhere(), anywhere()],
            out_specs=(vmem(), vmem(), vmem()),
            scratch_shapes=geno_scratch + [dma((len(PARTS),))],
            compiler_params=params,
            cost_estimate=cost(half, markers * feats * 2),
        )(genotypes, frequencies)
    to_chip = kept + lax.ppermute(to_core, "marker", OTHER_CORE)
    from_chip = lax.ppermute(to_chip, "marker", OTHER_CHIP)
    with jax.named_scope("projection_this_chip"):
        to_core, kept = pl.pallas_call(
            second_kernel,
            out_shape=(part, part),
            in_specs=[anywhere(), vmem(), anywhere()],
            out_specs=(vmem(), vmem()),
            scratch_shapes=geno_scratch,
            compiler_params=params,
            cost_estimate=cost(half),
        )(genotypes, panel, to_chip)
    from_core = lax.ppermute(to_core, "marker", OTHER_CORE)
    with jax.named_scope("features"):
        features = pl.pallas_call(
            features_kernel,
            out_shape=jax.ShapeDtypeStruct((quarter, feats), jnp.bfloat16),
            in_specs=[vmem()] * 3,
            out_specs=vmem(),
            compiler_params=small,
        )(kept + from_chip, from_core, phases.reshape(1, feats))
    features_other = lax.ppermute(features, "marker", OTHER_CORE)
    with jax.named_scope("gram_cross"):
        partial_sums = pl.pallas_call(
            gram_kernel,
            out_shape=jax.ShapeDtypeStruct((feats, feats // 2 + traits), jnp.bfloat16),
            in_specs=[vmem()] * 3,
            out_specs=vmem(),
            compiler_params=small,
        )(features, features_other, phenotypes)
    pieces = lax.all_to_all(partial_sums, "animal", 0, 0, tiled=True)
    with jax.named_scope("sum_animals"):
        own = pl.pallas_call(
            functools.partial(sum_kernel, groups),
            out_shape=jax.ShapeDtypeStruct((feats // groups, feats // 2 + traits), jnp.float32),
            in_specs=[vmem()],
            out_specs=vmem(),
            compiler_params=small,
        )(pieces)
    others = [lax.ppermute(own, "marker", pairs) for pairs in (OTHER_CORE, OTHER_CHIP, OTHER_BOTH)]
    with jax.named_scope("finish"):
        return pl.pallas_call(
            functools.partial(finish_kernel, animals_all),
            out_shape=(
                jax.ShapeDtypeStruct((feats // groups, feats), jnp.float32),
                jax.ShapeDtypeStruct((feats // groups, traits), jnp.float32),
            ),
            in_specs=[vmem()] * 4,
            out_specs=(vmem(), vmem()),
            compiler_params=small,
        )(own, *others)


def solution(mesh):
    in_specs = (P("animal", "marker"), P("marker", None), P(), P("animal", None))
    out_specs = (P("animal", None), P("animal", None))
    return jax.shard_map(
        on_device, mesh=mesh, in_specs=in_specs, out_specs=out_specs, check_vma=False
    )
```

```python
import functools
import math

import jax
import jax.numpy as jnp
from jax import lax
from jax.experimental import pallas as pl
from jax.experimental.pallas import tpu as pltpu
from jax.sharding import PartitionSpec as P

OTHER_CORE = [(0, 1), (1, 0), (2, 3), (3, 2)]
OTHER_CHIP = [(0, 2), (2, 0), (1, 3), (3, 1)]
TILE = 256
PARTS = [(0, 512), (512, 512)] + [(1024 * k, 1024) for k in range(1, 7)] + [(7168, 512), (7680, 512)]
AHEAD = (0, 7, 4, 4)
SINE = (-8.88576566829991, 58.46592923637672, -115.4012466635561, 108.25774031408996, -55.913345915340486)


def to_turns(radians):
    steps = jnp.round(radians * (65536.0 / (2.0 * math.pi))).astype(jnp.int32)
    return ((steps << 16) >> 16).astype(jnp.int16)


def copies(geno_hbm, first, geno, sem, parts):
    rows = geno.shape[0]
    return {
        step: pltpu.make_async_copy(
            geno_hbm.at[pl.ds(pl.multiple_of(first, 32), rows), pl.ds(PARTS[step][0], PARTS[step][1])],
            geno.at[:, pl.ds(PARTS[step][0], PARTS[step][1])],
            sem.at[step],
        )
        for step in parts
    }


def row_of(block):
    place = lax.axis_index("marker")
    chip, core = place // 2, place % 2
    other_chip, other_core, quarter_rows, offset, _ = block
    chip = 1 - chip if other_chip else chip
    core = 1 - core if other_core else core
    return (chip * 2 + core) * quarter_rows + offset


def projection_kernel(block, came_parts, next_block, next_parts, loads_panel, *refs):
    refs = list(refs)
    geno_hbm, panel_in = refs.pop(0), refs.pop(0)
    came_ref = refs.pop(0) if came_parts else None
    if not loads_panel:
        refs.pop(0)
    out_ref = refs.pop(0)
    panel_ref = refs.pop(0) if loads_panel else panel_in
    ahead_ref = refs.pop(0) if next_parts else None
    geno, geno_sem, ahead_sem, panel_sem = refs
    came_cols = PARTS[came_parts][0]
    geno_copies = copies(geno_hbm, row_of(block), geno, geno_sem, range(came_parts, len(PARTS)))
    panel_copies = []
    if loads_panel:
        panel_copies = [
            pltpu.make_async_copy(panel_in.at[pl.ds(start, width)], panel_ref.at[pl.ds(start, width)], panel_sem.at[step])
            for step, (start, width) in enumerate(PARTS)
        ]
    ahead_copies = copies(geno_hbm, row_of(next_block), ahead_ref, ahead_sem, range(next_parts)) if next_parts else {}
    for step in range(len(PARTS)):
        if loads_panel:
            panel_copies[step].start()
        if step >= came_parts:
            geno_copies[step].start()
    for copy in ahead_copies.values():
        copy.start()

    def run(*sums):
        for step, (start, width) in enumerate(PARTS):
            if loads_panel:
                panel_copies[step].wait()
            if step >= came_parts:
                geno_copies[step].wait()
            for tile in range(start, start + width, TILE):
                source = came_ref if tile < came_cols else geno
                dosage = (source[:, tile : tile + TILE] - 1).astype(jnp.float32).astype(jnp.bfloat16)
                slot = tile // TILE % 2
                for unit in range(2):
                    pltpu.matmul_push_rhs(panel_ref[tile : tile + TILE, unit * TILE : (unit + 1) * TILE], slot, unit)
                for unit in range(2):
                    pltpu.matmul_acc_lhs(sums[unit], dosage, slot)
        for unit in range(2):
            out_ref[:, unit * TILE : (unit + 1) * TILE] = to_turns(pltpu.matmul_pop(sums[unit]))

    pl.run_scoped(run, *[pltpu.ACC(unit)((geno.shape[0], TILE), jnp.float32) for unit in range(2)])
    for copy in ahead_copies.values():
        copy.wait()


def projection(blocks, ahead, step, geno, panel, came, after=()):
    block, loads_panel = blocks[step], step == 0
    last = step == len(blocks) - 1
    rows, markers, feats = block[-1], geno.shape[1], panel.shape[1]
    next_parts = 0 if last else ahead[step + 1]
    outs = [jax.ShapeDtypeStruct((rows, feats), jnp.int16)]
    if loads_panel:
        outs.append(pltpu.VMEM((markers, feats), jnp.bfloat16))
    if next_parts:
        outs.append(pltpu.VMEM((blocks[step + 1][-1], PARTS[next_parts][0]), jnp.int32))
    operands = [geno, panel] + ([came] if ahead[step] else []) + list(after)
    sems = pltpu.SemaphoreType.DMA((len(PARTS),))
    scratch = rows * markers * 4
    with jax.named_scope(f"projection_block_{step}"):
        made = pl.pallas_call(
            functools.partial(projection_kernel, block, ahead[step], None if last else blocks[step + 1], next_parts, loads_panel),
            out_shape=tuple(outs),
            in_specs=[anywhere(), anywhere() if loads_panel else vmem()] + [vmem()] * bool(ahead[step]) + [anywhere()] * len(after),
            out_specs=(vmem(),) * len(outs),
            scratch_shapes=[pltpu.VMEM((rows, markers), jnp.int32), sems, sems, sems],
            compiler_params=pltpu.CompilerParams(vmem_limit_bytes=scratch + 6 * 2**20),
            cost_estimate=pl.CostEstimate(
                flops=2 * rows * markers * feats, bytes_accessed=scratch + loads_panel * markers * feats * 2, transcendentals=0
            ),
        )(*operands)
    made = list(made)
    return made[0], made[1] if loads_panel else panel, made[-1] if next_parts else None


def features_kernel(kept_ref, core_ref, phase_ref, out_ref):
    turns = kept_ref[...].astype(jnp.int32) + core_ref[...].astype(jnp.int32)
    turns = ((turns << 16) >> 16).astype(jnp.float32) * (1.0 / 65536.0)
    turns = turns + phase_ref[...] * (1.0 / (2.0 * math.pi))
    turns = turns - jnp.round(turns)
    t = jnp.abs(turns) - 0.25
    square = t * t
    value = jnp.full_like(t, SINE[-1])
    for factor in SINE[-2::-1]:
        value = value * square + factor
    out_ref[...] = (value * t).astype(jnp.bfloat16)


def gram_kernel(from_other_core, feature_ref, pheno_ref, *refs):
    out_ref = refs[-1]
    rows, feats = feature_ref.shape
    half = feats // 2
    place = lax.axis_index("marker")
    core = place % 2
    spot = place + 1 - 2 * core if from_other_core else place
    features = feature_ref[...]
    phenotypes = pheno_ref[pl.ds(pl.multiple_of(spot * rows, rows), rows)]

    def product(right):
        return lax.dot_general(features, right, (((0,), (0,)), ((), ())), preferred_element_type=jnp.float32)

    gram = product(feature_ref[:, pl.ds(pl.multiple_of(core * half, half), half)])
    cross = product(phenotypes)
    if not from_other_core:
        out_ref[:, :half] = gram
        out_ref[:, half:] = cross
        return
    gram = gram + refs[0][:, :half]
    cross = cross + refs[0][:, half:]
    high = cross.astype(jnp.bfloat16)
    low = (cross - high.astype(jnp.float32)).astype(jnp.bfloat16)
    out_ref[:, :half] = gram.astype(jnp.bfloat16)
    out_ref[:, half:] = jnp.where(core == 0, high, low)


def sum_kernel(parts, in_ref, out_ref):
    wide = in_ref[...].astype(jnp.float32)
    out_ref[...] = jnp.sum(wide.reshape(parts, wide.shape[0] // parts, wide.shape[1]), axis=0)


def join_kernel(own_ref, other_ref, out_ref):
    core = lax.axis_index("marker") % 2
    out_ref[core] = own_ref[...]
    out_ref[1 - core] = other_ref[...]


def finish_kernel(animals_all, here_ref, there_ref, gram_ref, cross_ref):
    half = gram_ref.shape[1] // 2
    total = here_ref[...] + there_ref[...]
    gram_ref[:, :half] = total[0, :, :half] / animals_all
    gram_ref[:, half:] = total[1, :, :half] / animals_all
    cross_ref[...] = (total[0, :, half:] + total[1, :, half:]) / math.sqrt(animals_all)


def vmem():
    return pl.BlockSpec(memory_space=pltpu.VMEM)


def anywhere():
    return pl.BlockSpec(memory_space=pl.ANY)


def on_device(genotypes, frequencies, phases, phenotypes):
    rows, markers = genotypes.shape
    feats = frequencies.shape[1]
    traits = phenotypes.shape[1]
    groups = lax.axis_size("animal")
    animals_all = float(groups * rows)
    quarter = rows // 4
    small = pltpu.CompilerParams(vmem_limit_bytes=12 * 2**20)
    genotypes = pltpu.with_memory_space_constraint(genotypes, pltpu.HBM)
    frequencies = pltpu.with_memory_space_constraint(frequencies, pltpu.HBM)

    blocks = [(True, True, quarter, 0, quarter), (True, False, quarter, 0, quarter), (False, True, quarter, 0, quarter), (False, False, quarter, 0, quarter)]
    to_core, panel, ahead = projection(blocks, AHEAD, 0, genotypes, frequencies, None)
    received = lax.ppermute(to_core, "marker", OTHER_CORE)
    kept, panel, ahead = projection(blocks, AHEAD, 1, genotypes, panel, ahead, (to_core,))
    to_chip = kept + received
    from_chip = lax.ppermute(to_chip, "marker", OTHER_CHIP)
    to_core, panel, ahead = projection(blocks, AHEAD, 2, genotypes, panel, ahead, (to_chip,))
    from_core = lax.ppermute(to_core, "marker", OTHER_CORE)
    kept, panel, ahead = projection(blocks, AHEAD, 3, genotypes, panel, ahead, (to_core,))
    with jax.named_scope("features"):
        features = pl.pallas_call(
            features_kernel,
            out_shape=jax.ShapeDtypeStruct((quarter, feats), jnp.bfloat16),
            in_specs=[vmem()] * 3,
            out_specs=vmem(),
            compiler_params=small,
        )(kept + from_chip, from_core, phases.reshape(1, feats))
    features_other = lax.ppermute(features, "marker", OTHER_CORE)

    def gram_of(kind, from_other_core, *operands):
        return pl.pallas_call(
            functools.partial(gram_kernel, from_other_core),
            out_shape=jax.ShapeDtypeStruct((feats, feats // 2 + traits), kind),
            in_specs=[vmem()] * len(operands),
            out_specs=vmem(),
            compiler_params=small,
            cost_estimate=pl.CostEstimate(flops=feats * quarter * (feats + 2 * traits), bytes_accessed=0, transcendentals=0),
        )(*operands)

    with jax.named_scope("gram_cross"):
        partial_sums = gram_of(jnp.float32, False, features, phenotypes)
        partial_sums = gram_of(jnp.bfloat16, True, features_other, phenotypes, partial_sums)
    pieces = lax.all_to_all(partial_sums, "animal", 0, 0, tiled=True)
    with jax.named_scope("sum_animals"):
        own = pl.pallas_call(
            functools.partial(sum_kernel, groups),
            out_shape=jax.ShapeDtypeStruct((feats // groups, feats // 2 + traits), jnp.float32),
            in_specs=[vmem()],
            out_specs=vmem(),
            compiler_params=small,
        )(pieces)
    other = lax.ppermute(own, "marker", OTHER_CORE)
    with jax.named_scope("join_cores"):
        here = pl.pallas_call(
            join_kernel,
            out_shape=jax.ShapeDtypeStruct((2,) + own.shape, jnp.float32),
            in_specs=[vmem()] * 2,
            out_specs=vmem(),
            compiler_params=small,
        )(own, other)
    there = lax.ppermute(here, "marker", OTHER_CHIP)
    with jax.named_scope("finish"):
        return pl.pallas_call(
            functools.partial(finish_kernel, animals_all),
            out_shape=(
                jax.ShapeDtypeStruct((feats // groups, feats), jnp.float32),
                jax.ShapeDtypeStruct((feats // groups, traits), jnp.float32),
            ),
            in_specs=[vmem()] * 2,
            out_specs=(vmem(), vmem()),
            compiler_params=small,
        )(here, there)


def solution(mesh):
    in_specs = (P("animal", "marker"), P("marker", None), P(), P("animal", None))
    out_specs = (P("animal", None), P("animal", None))
    return jax.shard_map(
        on_device, mesh=mesh, in_specs=in_specs, out_specs=out_specs, check_vma=False
    )
```

```python
import functools
import math

import jax
import jax.numpy as jnp
from jax import lax
from jax.experimental import pallas as pl
from jax.experimental.pallas import tpu as pltpu
from jax.sharding import PartitionSpec as P

OTHER_CORE = [(0, 1), (1, 0), (2, 3), (3, 2)]
OTHER_CHIP = [(0, 2), (2, 0), (1, 3), (3, 1)]
TILE = 256
PARTS = [(0, 1024), (1024, 1024), (2048, 2048), (4096, 2048), (6144, 1536), (7680, 512)]
AHEAD = (0, 4, 2, 3)
SINE = (-8.88576566829991, 58.46592923637672, -115.4012466635561, 108.25774031408996, -55.913345915340486)


def to_turns(radians):
    steps = jnp.round(radians * (65536.0 / (2.0 * math.pi))).astype(jnp.int32)
    return ((steps << 16) >> 16).astype(jnp.int16)


def copies(geno_hbm, first, geno, sem, parts):
    rows = geno.shape[0]
    return {
        step: pltpu.make_async_copy(
            geno_hbm.at[pl.ds(pl.multiple_of(first, 32), rows), pl.ds(PARTS[step][0], PARTS[step][1])],
            geno.at[:, pl.ds(PARTS[step][0], PARTS[step][1])],
            sem.at[step],
        )
        for step in parts
    }


def row_of(block):
    place = lax.axis_index("marker")
    chip, core = place // 2, place % 2
    other_chip, other_core, quarter_rows, offset, _ = block
    chip = 1 - chip if other_chip else chip
    core = 1 - core if other_core else core
    return (chip * 2 + core) * quarter_rows + offset


def projection_kernel(block, came_parts, next_block, next_parts, loads_panel, *refs):
    refs = list(refs)
    geno_hbm, panel_in = refs.pop(0), refs.pop(0)
    came_ref = refs.pop(0) if came_parts else None
    if not loads_panel:
        refs.pop(0)
    out_ref = refs.pop(0)
    panel_ref = refs.pop(0) if loads_panel else panel_in
    ahead_ref = refs.pop(0) if next_parts else None
    geno, geno_sem, ahead_sem, panel_sem = refs
    came_cols = PARTS[came_parts][0]
    geno_copies = copies(geno_hbm, row_of(block), geno, geno_sem, range(came_parts, len(PARTS)))
    panel_copies = []
    if loads_panel:
        panel_copies = [
            pltpu.make_async_copy(panel_in.at[pl.ds(start, width)], panel_ref.at[pl.ds(start, width)], panel_sem.at[step])
            for step, (start, width) in enumerate(PARTS)
        ]
    ahead_copies = copies(geno_hbm, row_of(next_block), ahead_ref, ahead_sem, range(next_parts)) if next_parts else {}
    for step in range(len(PARTS)):
        if loads_panel:
            panel_copies[step].start()
        if step >= came_parts:
            geno_copies[step].start()
    for copy in ahead_copies.values():
        copy.start()

    def run(*sums):
        for step, (start, width) in enumerate(PARTS):
            if loads_panel:
                panel_copies[step].wait()
            if step >= came_parts:
                geno_copies[step].wait()
            for tile in range(start, start + width, TILE):
                source = came_ref if tile < came_cols else geno
                dosage = (source[:, tile : tile + TILE] - 1).astype(jnp.float32).astype(jnp.bfloat16)
                slot = tile // TILE % 2
                for unit in range(2):
                    pltpu.matmul_push_rhs(panel_ref[tile : tile + TILE, unit * TILE : (unit + 1) * TILE], slot, unit)
                for unit in range(2):
                    pltpu.matmul_acc_lhs(sums[unit], dosage, slot)
        for unit in range(2):
            out_ref[:, unit * TILE : (unit + 1) * TILE] = to_turns(pltpu.matmul_pop(sums[unit]))

    pl.run_scoped(run, *[pltpu.ACC(unit)((geno.shape[0], TILE), jnp.float32) for unit in range(2)])
    for copy in ahead_copies.values():
        copy.wait()


def projection(blocks, ahead, step, geno, panel, came, after=()):
    block, loads_panel = blocks[step], step == 0
    last = step == len(blocks) - 1
    rows, markers, feats = block[-1], geno.shape[1], panel.shape[1]
    next_parts = 0 if last else ahead[step + 1]
    outs = [jax.ShapeDtypeStruct((rows, feats), jnp.int16)]
    if loads_panel:
        outs.append(pltpu.VMEM((markers, feats), jnp.bfloat16))
    if next_parts:
        outs.append(pltpu.VMEM((blocks[step + 1][-1], PARTS[next_parts][0]), jnp.int32))
    operands = [geno, panel] + ([came] if ahead[step] else []) + list(after)
    sems = pltpu.SemaphoreType.DMA((len(PARTS),))
    scratch = rows * markers * 4
    with jax.named_scope(f"projection_block_{step}"):
        made = pl.pallas_call(
            functools.partial(projection_kernel, block, ahead[step], None if last else blocks[step + 1], next_parts, loads_panel),
            out_shape=tuple(outs),
            in_specs=[anywhere(), anywhere() if loads_panel else vmem()] + [vmem()] * bool(ahead[step]) + [anywhere()] * len(after),
            out_specs=(vmem(),) * len(outs),
            scratch_shapes=[pltpu.VMEM((rows, markers), jnp.int32), sems, sems, sems],
            compiler_params=pltpu.CompilerParams(vmem_limit_bytes=scratch + 6 * 2**20),
            cost_estimate=pl.CostEstimate(
                flops=2 * rows * markers * feats, bytes_accessed=scratch + loads_panel * markers * feats * 2, transcendentals=0
            ),
        )(*operands)
    made = list(made)
    return made[0], made[1] if loads_panel else panel, made[-1] if next_parts else None


def features_kernel(kept_ref, core_ref, phase_ref, out_ref):
    turns = kept_ref[...].astype(jnp.int32) + core_ref[...].astype(jnp.int32)
    turns = ((turns << 16) >> 16).astype(jnp.float32) * (1.0 / 65536.0)
    turns = turns + phase_ref[...] * (1.0 / (2.0 * math.pi))
    turns = turns - jnp.round(turns)
    t = jnp.abs(turns) - 0.25
    square = t * t
    value = jnp.full_like(t, SINE[-1])
    for factor in SINE[-2::-1]:
        value = value * square + factor
    out_ref[...] = (value * t).astype(jnp.bfloat16)


def gram_kernel(from_other_core, feature_ref, pheno_ref, *refs):
    out_ref = refs[-1]
    rows, feats = feature_ref.shape
    half = feats // 2
    place = lax.axis_index("marker")
    core = place % 2
    spot = place + 1 - 2 * core if from_other_core else place
    features = feature_ref[...]
    phenotypes = pheno_ref[pl.ds(pl.multiple_of(spot * rows, rows), rows)]

    def product(right):
        return lax.dot_general(features, right, (((0,), (0,)), ((), ())), preferred_element_type=jnp.float32)

    gram = product(feature_ref[:, pl.ds(pl.multiple_of(core * half, half), half)])
    cross = product(phenotypes)
    if not from_other_core:
        out_ref[:, :half] = gram
        out_ref[:, half:] = cross
        return
    gram = gram + refs[0][:, :half]
    cross = cross + refs[0][:, half:]
    high = cross.astype(jnp.bfloat16)
    low = (cross - high.astype(jnp.float32)).astype(jnp.bfloat16)
    out_ref[:, :half] = gram.astype(jnp.bfloat16)
    out_ref[:, half:] = jnp.where(core == 0, high, low)


def sum_kernel(parts, in_ref, out_ref):
    wide = in_ref[...].astype(jnp.float32)
    out_ref[...] = jnp.sum(wide.reshape(parts, wide.shape[0] // parts, wide.shape[1]), axis=0)


def join_kernel(own_ref, other_ref, out_ref):
    core = lax.axis_index("marker") % 2
    out_ref[core] = own_ref[...]
    out_ref[1 - core] = other_ref[...]


def finish_kernel(animals_all, here_ref, there_ref, gram_ref, cross_ref):
    half = gram_ref.shape[1] // 2
    total = here_ref[...] + there_ref[...]
    gram_ref[:, :half] = total[0, :, :half] / animals_all
    gram_ref[:, half:] = total[1, :, :half] / animals_all
    cross_ref[...] = (total[0, :, half:] + total[1, :, half:]) / math.sqrt(animals_all)


def vmem():
    return pl.BlockSpec(memory_space=pltpu.VMEM)


def anywhere():
    return pl.BlockSpec(memory_space=pl.ANY)


def on_device(genotypes, frequencies, phases, phenotypes):
    rows, markers = genotypes.shape
    feats = frequencies.shape[1]
    traits = phenotypes.shape[1]
    groups = lax.axis_size("animal")
    animals_all = float(groups * rows)
    quarter = rows // 4
    small = pltpu.CompilerParams(vmem_limit_bytes=12 * 2**20)
    genotypes = pltpu.with_memory_space_constraint(genotypes, pltpu.HBM)
    frequencies = pltpu.with_memory_space_constraint(frequencies, pltpu.HBM)

    blocks = [(True, True, quarter, 0, quarter), (True, False, quarter, 0, quarter), (False, True, quarter, 0, quarter), (False, False, quarter, 0, quarter)]
    to_core, panel, ahead = projection(blocks, AHEAD, 0, genotypes, frequencies, None)
    received = lax.ppermute(to_core, "marker", OTHER_CORE)
    kept, panel, ahead = projection(blocks, AHEAD, 1, genotypes, panel, ahead, (to_core,))
    to_chip = kept + received
    from_chip = lax.ppermute(to_chip, "marker", OTHER_CHIP)
    to_core, panel, ahead = projection(blocks, AHEAD, 2, genotypes, panel, ahead, (to_chip,))
    from_core = lax.ppermute(to_core, "marker", OTHER_CORE)
    kept, panel, ahead = projection(blocks, AHEAD, 3, genotypes, panel, ahead, (to_core,))
    with jax.named_scope("features"):
        features = pl.pallas_call(
            features_kernel,
            out_shape=jax.ShapeDtypeStruct((quarter, feats), jnp.bfloat16),
            in_specs=[vmem()] * 3,
            out_specs=vmem(),
            compiler_params=small,
        )(kept + from_chip, from_core, phases.reshape(1, feats))
    features_other = lax.ppermute(features, "marker", OTHER_CORE)

    def gram_of(kind, from_other_core, *operands):
        return pl.pallas_call(
            functools.partial(gram_kernel, from_other_core),
            out_shape=jax.ShapeDtypeStruct((feats, feats // 2 + traits), kind),
            in_specs=[vmem()] * len(operands),
            out_specs=vmem(),
            compiler_params=small,
            cost_estimate=pl.CostEstimate(flops=feats * quarter * (feats + 2 * traits), bytes_accessed=0, transcendentals=0),
        )(*operands)

    with jax.named_scope("gram_cross"):
        partial_sums = gram_of(jnp.float32, False, features, phenotypes)
        partial_sums = gram_of(jnp.bfloat16, True, features_other, phenotypes, partial_sums)
    pieces = lax.all_to_all(partial_sums, "animal", 0, 0, tiled=True)
    with jax.named_scope("sum_animals"):
        own = pl.pallas_call(
            functools.partial(sum_kernel, groups),
            out_shape=jax.ShapeDtypeStruct((feats // groups, feats // 2 + traits), jnp.float32),
            in_specs=[vmem()],
            out_specs=vmem(),
            compiler_params=small,
        )(pieces)
    other = lax.ppermute(own, "marker", OTHER_CORE)
    with jax.named_scope("join_cores"):
        here = pl.pallas_call(
            join_kernel,
            out_shape=jax.ShapeDtypeStruct((2,) + own.shape, jnp.float32),
            in_specs=[vmem()] * 2,
            out_specs=vmem(),
            compiler_params=small,
        )(own, other)
    there = lax.ppermute(here, "marker", OTHER_CHIP)
    with jax.named_scope("finish"):
        return pl.pallas_call(
            functools.partial(finish_kernel, animals_all),
            out_shape=(
                jax.ShapeDtypeStruct((feats // groups, feats), jnp.float32),
                jax.ShapeDtypeStruct((feats // groups, traits), jnp.float32),
            ),
            in_specs=[vmem()] * 2,
            out_specs=(vmem(), vmem()),
            compiler_params=small,
        )(here, there)


def solution(mesh):
    in_specs = (P("animal", "marker"), P("marker", None), P(), P("animal", None))
    out_specs = (P("animal", None), P("animal", None))
    return jax.shard_map(
        on_device, mesh=mesh, in_specs=in_specs, out_specs=out_specs, check_vma=False
    )
```

```python
import functools
import math

import jax
import jax.numpy as jnp
from jax import lax
from jax.experimental import pallas as pl
from jax.experimental.pallas import tpu as pltpu
from jax.sharding import PartitionSpec as P

OTHER_CORE = [(0, 1), (1, 0), (2, 3), (3, 2)]
OTHER_CHIP = [(0, 2), (2, 0), (1, 3), (3, 1)]
TILE = 256
LANES = 128
PARTS = [(0, 1024), (1024, 1024), (2048, 2048), (4096, 2048), (6144, 1536), (7680, 512)]
AHEAD = (0, 4, 2, 3)
SINE = (-8.88576566829991, 58.46592923637672, -115.4012466635561, 108.25774031408996, -55.913345915340486)


def to_turns(radians):
    steps = jnp.round(radians * (65536.0 / (2.0 * math.pi))).astype(jnp.int32)
    return ((steps << 16) >> 16).astype(jnp.int16)


def copies(geno_hbm, first, geno, sem, parts):
    rows = geno.shape[0]
    return {
        step: pltpu.make_async_copy(
            geno_hbm.at[pl.ds(pl.multiple_of(first, 32), rows), pl.ds(PARTS[step][0], PARTS[step][1])],
            geno.at[:, pl.ds(PARTS[step][0], PARTS[step][1])],
            sem.at[step],
        )
        for step in parts
    }


def row_of(block):
    place = lax.axis_index("marker")
    chip, core = place // 2, place % 2
    other_chip, other_core, quarter_rows, offset, _ = block
    chip = 1 - chip if other_chip else chip
    core = 1 - core if other_core else core
    return (chip * 2 + core) * quarter_rows + offset


def projection_kernel(block, came_parts, next_block, next_parts, loads_panel, *refs):
    refs = list(refs)
    geno_hbm, panel_in = refs.pop(0), refs.pop(0)
    came_ref = refs.pop(0) if came_parts else None
    if not loads_panel:
        refs.pop(0)
    out_ref = refs.pop(0)
    panel_ref = refs.pop(0) if loads_panel else panel_in
    ahead_ref = refs.pop(0) if next_parts else None
    geno, geno_sem, ahead_sem, panel_sem = refs
    came_cols = PARTS[came_parts][0]
    geno_copies = copies(geno_hbm, row_of(block), geno, geno_sem, range(came_parts, len(PARTS)))
    panel_copies = []
    if loads_panel:
        panel_copies = [
            pltpu.make_async_copy(panel_in.at[pl.ds(start, width)], panel_ref.at[pl.ds(start, width)], panel_sem.at[step])
            for step, (start, width) in enumerate(PARTS)
        ]
    ahead_copies = copies(geno_hbm, row_of(next_block), ahead_ref, ahead_sem, range(next_parts)) if next_parts else {}
    for step in range(len(PARTS)):
        if loads_panel:
            panel_copies[step].start()
        if step >= came_parts:
            geno_copies[step].start()
    for copy in ahead_copies.values():
        copy.start()

    def run(*sums):
        for step, (start, width) in enumerate(PARTS):
            if loads_panel:
                panel_copies[step].wait()
            if step >= came_parts:
                geno_copies[step].wait()
            for tile in range(start, start + width, TILE):
                source = came_ref if tile < came_cols else geno
                dosage = (source[:, tile : tile + TILE] - 1).astype(jnp.float32).astype(jnp.bfloat16)
                slot = tile // TILE % 2
                for unit in range(2):
                    pltpu.matmul_push_rhs(panel_ref[tile : tile + TILE, unit * TILE : (unit + 1) * TILE], slot, unit)
                for unit in range(2):
                    pltpu.matmul_acc_lhs(sums[unit], dosage, slot)
        for unit in range(2):
            out_ref[:, unit * TILE : (unit + 1) * TILE] = to_turns(pltpu.matmul_pop(sums[unit]))

    pl.run_scoped(run, *[pltpu.ACC(unit)((geno.shape[0], TILE), jnp.float32) for unit in range(2)])
    for copy in ahead_copies.values():
        copy.wait()


def projection(blocks, ahead, step, geno, panel, came, after=()):
    block, loads_panel = blocks[step], step == 0
    last = step == len(blocks) - 1
    rows, markers, feats = block[-1], geno.shape[1], panel.shape[1]
    next_parts = 0 if last else ahead[step + 1]
    outs = [jax.ShapeDtypeStruct((rows, feats), jnp.int16)]
    if loads_panel:
        outs.append(pltpu.VMEM((markers, feats), jnp.bfloat16))
    if next_parts:
        outs.append(pltpu.VMEM((blocks[step + 1][-1], PARTS[next_parts][0]), jnp.int32))
    operands = [geno, panel] + ([came] if ahead[step] else []) + list(after)
    sems = pltpu.SemaphoreType.DMA((len(PARTS),))
    scratch = rows * markers * 4
    with jax.named_scope(f"projection_block_{step}"):
        made = pl.pallas_call(
            functools.partial(projection_kernel, block, ahead[step], None if last else blocks[step + 1], next_parts, loads_panel),
            out_shape=tuple(outs),
            in_specs=[anywhere(), anywhere() if loads_panel else vmem()] + [vmem()] * bool(ahead[step]) + [anywhere()] * len(after),
            out_specs=(vmem(),) * len(outs),
            scratch_shapes=[pltpu.VMEM((rows, markers), jnp.int32), sems, sems, sems],
            compiler_params=pltpu.CompilerParams(vmem_limit_bytes=scratch + 6 * 2**20),
            cost_estimate=pl.CostEstimate(
                flops=2 * rows * markers * feats, bytes_accessed=scratch + loads_panel * markers * feats * 2, transcendentals=0
            ),
        )(*operands)
    made = list(made)
    return made[0], made[1] if loads_panel else panel, made[-1] if next_parts else None


def features_kernel(kept_ref, core_ref, phase_ref, out_ref):
    turns = kept_ref[...].astype(jnp.int32) + core_ref[...].astype(jnp.int32)
    turns = ((turns << 16) >> 16).astype(jnp.float32) * (1.0 / 65536.0)
    turns = turns + phase_ref[...] * (1.0 / (2.0 * math.pi))
    turns = turns - jnp.round(turns)
    t = jnp.abs(turns) - 0.25
    square = t * t
    value = jnp.full_like(t, SINE[-1])
    for factor in SINE[-2::-1]:
        value = value * square + factor
    out_ref[...] = (value * t).astype(jnp.bfloat16)


def gram_kernel(from_other_core, feature_ref, pheno_ref, *refs):
    out_ref = refs[-1]
    rows, feats = feature_ref.shape
    half = feats // 2
    place = lax.axis_index("marker")
    core = place % 2
    spot = place + 1 - 2 * core if from_other_core else place
    features = feature_ref[...]
    phenotypes = pheno_ref[pl.ds(pl.multiple_of(spot * rows, rows), rows)]

    def product(right):
        return lax.dot_general(features, right, (((0,), (0,)), ((), ())), preferred_element_type=jnp.float32)

    gram = product(feature_ref[:, pl.ds(pl.multiple_of(core * half, half), half)])
    cross = product(phenotypes)
    if not from_other_core:
        out_ref[:, :half] = gram
        out_ref[:, half:] = cross
        return
    pieces = out_ref.shape[0]
    height = feats // pieces
    gram = (gram + refs[0][:, :half]).astype(jnp.bfloat16)
    cross = (cross + refs[0][:, half:]).reshape(pieces, 2, height // 2, LANES)
    left = lax.broadcasted_iota(jnp.int32, (pieces, height // 2, LANES), 2) < LANES // 2
    cross = jnp.where(left, cross[:, 0], cross[:, 1])
    high = cross.astype(jnp.bfloat16)
    low = (cross - high.astype(jnp.float32)).astype(jnp.bfloat16)
    out_ref[:, :height] = gram[:, :LANES].reshape(pieces, height, LANES)
    out_ref[:, height : 2 * height] = gram[:, LANES:].reshape(pieces, height, LANES)
    out_ref[:, 2 * height :] = jnp.where(core == 0, high, low)


def sum_kernel(in_ref, out_ref):
    out_ref[...] = jnp.sum(in_ref[...].astype(jnp.float32), axis=0)


def join_kernel(own_ref, other_ref, out_ref):
    core = lax.axis_index("marker") % 2
    out_ref[core] = own_ref[...]
    out_ref[1 - core] = other_ref[...]


def finish_kernel(animals_all, here_ref, there_ref, gram_ref, cross_ref):
    height = gram_ref.shape[0]
    total = here_ref[...] + there_ref[...]
    for core in range(2):
        for part in range(2):
            start = (2 * core + part) * LANES
            gram_ref[:, start : start + LANES] = total[core, part * height : (part + 1) * height] / animals_all
    cross = (total[0, 2 * height :] + total[1, 2 * height :]) / math.sqrt(animals_all)
    cross_ref[: height // 2] = cross[:, : LANES // 2]
    cross_ref[height // 2 :] = cross[:, LANES // 2 :]


def vmem():
    return pl.BlockSpec(memory_space=pltpu.VMEM)


def anywhere():
    return pl.BlockSpec(memory_space=pl.ANY)


def on_device(genotypes, frequencies, phases, phenotypes):
    rows, markers = genotypes.shape
    feats = frequencies.shape[1]
    traits = phenotypes.shape[1]
    groups = lax.axis_size("animal")
    animals_all = float(groups * rows)
    quarter = rows // 4
    small = pltpu.CompilerParams(vmem_limit_bytes=12 * 2**20)
    genotypes = pltpu.with_memory_space_constraint(genotypes, pltpu.HBM)
    frequencies = pltpu.with_memory_space_constraint(frequencies, pltpu.HBM)

    blocks = [(True, True, quarter, 0, quarter), (True, False, quarter, 0, quarter), (False, True, quarter, 0, quarter), (False, False, quarter, 0, quarter)]
    to_core, panel, ahead = projection(blocks, AHEAD, 0, genotypes, frequencies, None)
    received = lax.ppermute(to_core, "marker", OTHER_CORE)
    kept, panel, ahead = projection(blocks, AHEAD, 1, genotypes, panel, ahead, (to_core,))
    to_chip = kept + received
    from_chip = lax.ppermute(to_chip, "marker", OTHER_CHIP)
    to_core, panel, ahead = projection(blocks, AHEAD, 2, genotypes, panel, ahead, (to_chip,))
    from_core = lax.ppermute(to_core, "marker", OTHER_CORE)
    kept, panel, ahead = projection(blocks, AHEAD, 3, genotypes, panel, ahead, (to_core,))
    with jax.named_scope("features"):
        features = pl.pallas_call(
            features_kernel,
            out_shape=jax.ShapeDtypeStruct((quarter, feats), jnp.bfloat16),
            in_specs=[vmem()] * 3,
            out_specs=vmem(),
            compiler_params=small,
        )(kept + from_chip, from_core, phases.reshape(1, feats))
    features_other = lax.ppermute(features, "marker", OTHER_CORE)

    height = feats // groups
    piece = (2 * height + height // 2, LANES)

    def gram_of(from_other_core, out_shape, *operands):
        return pl.pallas_call(
            functools.partial(gram_kernel, from_other_core),
            out_shape=out_shape,
            in_specs=[vmem()] * len(operands),
            out_specs=vmem(),
            compiler_params=small,
            cost_estimate=pl.CostEstimate(flops=feats * quarter * (feats + 2 * LANES), bytes_accessed=0, transcendentals=0),
        )(*operands)

    with jax.named_scope("gram_cross"):
        twice = jnp.concatenate([phenotypes, phenotypes], axis=1)
        partial_sums = gram_of(False, jax.ShapeDtypeStruct((feats, feats // 2 + LANES), jnp.float32), features, twice)
        partial_sums = gram_of(
            True, jax.ShapeDtypeStruct((groups,) + piece, jnp.bfloat16), features_other, twice, partial_sums
        )
    pieces = lax.all_to_all(partial_sums, "animal", 0, 0)
    with jax.named_scope("sum_animals"):
        own = pl.pallas_call(
            sum_kernel,
            out_shape=jax.ShapeDtypeStruct(piece, jnp.float32),
            in_specs=[vmem()],
            out_specs=vmem(),
            compiler_params=small,
        )(pieces)
    other = lax.ppermute(own, "marker", OTHER_CORE)
    with jax.named_scope("join_cores"):
        here = pl.pallas_call(
            join_kernel,
            out_shape=jax.ShapeDtypeStruct((2,) + own.shape, jnp.float32),
            in_specs=[vmem()] * 2,
            out_specs=vmem(),
            compiler_params=small,
        )(own, other)
    there = lax.ppermute(here, "marker", OTHER_CHIP)
    with jax.named_scope("finish"):
        return pl.pallas_call(
            functools.partial(finish_kernel, animals_all),
            out_shape=(
                jax.ShapeDtypeStruct((feats // groups, feats), jnp.float32),
                jax.ShapeDtypeStruct((feats // groups, traits), jnp.float32),
            ),
            in_specs=[vmem()] * 2,
            out_specs=(vmem(), vmem()),
            compiler_params=small,
        )(here, there)


def solution(mesh):
    in_specs = (P("animal", "marker"), P("marker", None), P(), P("animal", None))
    out_specs = (P("animal", None), P("animal", None))
    return jax.shard_map(
        on_device, mesh=mesh, in_specs=in_specs, out_specs=out_specs, check_vma=False
    )
```

```python
import functools
import math

import jax
import jax.numpy as jnp
from jax import lax
from jax.experimental import pallas as pl
from jax.experimental.pallas import tpu as pltpu
from jax.sharding import PartitionSpec as P

OTHER_CORE = [(0, 1), (1, 0), (2, 3), (3, 2)]
OTHER_CHIP = [(0, 2), (2, 0), (1, 3), (3, 1)]
TILE = 256
LANES = 128
PARTS = [(0, 1024), (1024, 1024), (2048, 2048), (4096, 2048), (6144, 1536), (7680, 512)]
AHEAD = (0, 4, 2, 3)
SINE = (-8.88576566829991, 58.46592923637672, -115.4012466635561, 108.25774031408996, -55.913345915340486)


def to_turns(radians):
    steps = jnp.round(radians * (65536.0 / (2.0 * math.pi))).astype(jnp.int32)
    return ((steps << 16) >> 16).astype(jnp.int16)


def copies(geno_hbm, first, geno, sem, parts):
    rows = geno.shape[0]
    return {
        step: pltpu.make_async_copy(
            geno_hbm.at[pl.ds(pl.multiple_of(first, 32), rows), pl.ds(PARTS[step][0], PARTS[step][1])],
            geno.at[:, pl.ds(PARTS[step][0], PARTS[step][1])],
            sem.at[step],
        )
        for step in parts
    }


def row_of(block):
    place = lax.axis_index("marker")
    chip, core = place // 2, place % 2
    other_chip, other_core, quarter_rows, offset, _ = block
    chip = 1 - chip if other_chip else chip
    core = 1 - core if other_core else core
    return (chip * 2 + core) * quarter_rows + offset


def projection_kernel(block, came_parts, next_block, next_parts, loads_panel, *refs):
    refs = list(refs)
    geno_hbm, panel_in = refs.pop(0), refs.pop(0)
    came_ref = refs.pop(0) if came_parts else None
    if not loads_panel:
        refs.pop(0)
    out_ref = refs.pop(0)
    panel_ref = refs.pop(0) if loads_panel else panel_in
    ahead_ref = refs.pop(0) if next_parts else None
    geno, geno_sem, ahead_sem, panel_sem = refs
    came_cols = PARTS[came_parts][0]
    geno_copies = copies(geno_hbm, row_of(block), geno, geno_sem, range(came_parts, len(PARTS)))
    panel_copies = []
    if loads_panel:
        panel_copies = [
            pltpu.make_async_copy(panel_in.at[pl.ds(start, width)], panel_ref.at[pl.ds(start, width)], panel_sem.at[step])
            for step, (start, width) in enumerate(PARTS)
        ]
    ahead_copies = copies(geno_hbm, row_of(next_block), ahead_ref, ahead_sem, range(next_parts)) if next_parts else {}
    for step in range(len(PARTS)):
        if loads_panel:
            panel_copies[step].start()
        if step >= came_parts:
            geno_copies[step].start()
    for copy in ahead_copies.values():
        copy.start()

    def run(*sums):
        for step, (start, width) in enumerate(PARTS):
            if loads_panel:
                panel_copies[step].wait()
            if step >= came_parts:
                geno_copies[step].wait()
            for tile in range(start, start + width, TILE):
                source = came_ref if tile < came_cols else geno
                dosage = (source[:, tile : tile + TILE] - 1).astype(jnp.float32).astype(jnp.bfloat16)
                slot = tile // TILE % 2
                for unit in range(2):
                    pltpu.matmul_push_rhs(panel_ref[tile : tile + TILE, unit * TILE : (unit + 1) * TILE], slot, unit)
                for unit in range(2):
                    pltpu.matmul_acc_lhs(sums[unit], dosage, slot)
        for unit in range(2):
            out_ref[:, unit * TILE : (unit + 1) * TILE] = to_turns(pltpu.matmul_pop(sums[unit]))

    pl.run_scoped(run, *[pltpu.ACC(unit)((geno.shape[0], TILE), jnp.float32) for unit in range(2)])
    for copy in ahead_copies.values():
        copy.wait()


def projection(blocks, ahead, step, geno, panel, came, after=()):
    block, loads_panel = blocks[step], step == 0
    last = step == len(blocks) - 1
    rows, markers, feats = block[-1], geno.shape[1], panel.shape[1]
    next_parts = 0 if last else ahead[step + 1]
    outs = [jax.ShapeDtypeStruct((rows, feats), jnp.int16)]
    if loads_panel:
        outs.append(pltpu.VMEM((markers, feats), jnp.bfloat16))
    if next_parts:
        outs.append(pltpu.VMEM((blocks[step + 1][-1], PARTS[next_parts][0]), jnp.int32))
    operands = [geno, panel] + ([came] if ahead[step] else []) + list(after)
    sems = pltpu.SemaphoreType.DMA((len(PARTS),))
    scratch = rows * markers * 4
    with jax.named_scope(f"projection_block_{step}"):
        made = pl.pallas_call(
            functools.partial(projection_kernel, block, ahead[step], None if last else blocks[step + 1], next_parts, loads_panel),
            out_shape=tuple(outs),
            in_specs=[anywhere(), anywhere() if loads_panel else vmem()] + [vmem()] * bool(ahead[step]) + [anywhere()] * len(after),
            out_specs=(vmem(),) * len(outs),
            scratch_shapes=[pltpu.VMEM((rows, markers), jnp.int32), sems, sems, sems],
            compiler_params=pltpu.CompilerParams(vmem_limit_bytes=scratch + 6 * 2**20),
            cost_estimate=pl.CostEstimate(
                flops=2 * rows * markers * feats, bytes_accessed=scratch + loads_panel * markers * feats * 2, transcendentals=0
            ),
        )(*operands)
    made = list(made)
    return made[0], made[1] if loads_panel else panel, made[-1] if next_parts else None


def features_kernel(kept_ref, core_ref, phase_ref, out_ref):
    turns = kept_ref[...].astype(jnp.int32) + core_ref[...].astype(jnp.int32)
    turns = ((turns << 16) >> 16).astype(jnp.float32) * (1.0 / 65536.0)
    turns = turns + phase_ref[...] * (1.0 / (2.0 * math.pi))
    turns = turns - jnp.round(turns)
    t = jnp.abs(turns) - 0.25
    square = t * t
    value = jnp.full_like(t, SINE[-1])
    for factor in SINE[-2::-1]:
        value = value * square + factor
    out_ref[...] = (value * t).astype(jnp.bfloat16)


def gram_kernel(from_other_core, feature_ref, pheno_ref, *refs):
    out_ref = refs[-1]
    rows, feats = feature_ref.shape
    half = feats // 2
    place = lax.axis_index("marker")
    core = place % 2
    spot = place + 1 - 2 * core if from_other_core else place
    features = feature_ref[...]
    phenotypes = pheno_ref[pl.ds(pl.multiple_of(spot * rows, rows), rows)]

    def product(right):
        return lax.dot_general(features, right, (((0,), (0,)), ((), ())), preferred_element_type=jnp.float32)

    gram = product(feature_ref[:, pl.ds(pl.multiple_of(core * half, half), half)])
    cross = product(phenotypes)
    if not from_other_core:
        out_ref[:, :half] = gram
        out_ref[:, half:] = cross
        return
    pieces = out_ref.shape[0]
    height = feats // pieces
    gram = (gram + refs[0][:, :half]).astype(jnp.bfloat16)
    cross = (cross + refs[0][:, half:]).reshape(pieces, 2, height // 2, LANES)
    left = lax.broadcasted_iota(jnp.int32, (pieces, height // 2, LANES), 2) < LANES // 2
    cross = jnp.where(left, cross[:, 0], cross[:, 1])
    high = cross.astype(jnp.bfloat16)
    low = (cross - high.astype(jnp.float32)).astype(jnp.bfloat16)
    halves = [gram[:, start : start + LANES].reshape(pieces, height, LANES) for start in (0, LANES)]
    out_ref[...] = jnp.concatenate(halves + [jnp.where(core == 0, high, low)], axis=1)


def sum_kernel(in_ref, out_ref):
    out_ref[...] = jnp.sum(in_ref[...].astype(jnp.float32), axis=0)


def join_kernel(own_ref, other_ref, out_ref):
    core = lax.axis_index("marker") % 2
    out_ref[core] = own_ref[...]
    out_ref[1 - core] = other_ref[...]


def finish_kernel(animals_all, here_ref, there_ref, gram_ref, cross_ref):
    height = gram_ref.shape[0]
    total = here_ref[...] + there_ref[...]
    for core in range(2):
        for part in range(2):
            start = (2 * core + part) * LANES
            gram_ref[:, start : start + LANES] = total[core, part * height : (part + 1) * height] / animals_all
    cross = (total[0, 2 * height :] + total[1, 2 * height :]) / math.sqrt(animals_all)
    cross_ref[: height // 2] = cross[:, : LANES // 2]
    cross_ref[height // 2 :] = cross[:, LANES // 2 :]


def vmem():
    return pl.BlockSpec(memory_space=pltpu.VMEM)


def anywhere():
    return pl.BlockSpec(memory_space=pl.ANY)


def on_device(genotypes, frequencies, phases, phenotypes):
    rows, markers = genotypes.shape
    feats = frequencies.shape[1]
    traits = phenotypes.shape[1]
    groups = lax.axis_size("animal")
    animals_all = float(groups * rows)
    quarter = rows // 4
    small = pltpu.CompilerParams(vmem_limit_bytes=12 * 2**20)
    genotypes = pltpu.with_memory_space_constraint(genotypes, pltpu.HBM)
    frequencies = pltpu.with_memory_space_constraint(frequencies, pltpu.HBM)

    blocks = [(True, True, quarter, 0, quarter), (True, False, quarter, 0, quarter), (False, True, quarter, 0, quarter), (False, False, quarter, 0, quarter)]
    to_core, panel, ahead = projection(blocks, AHEAD, 0, genotypes, frequencies, None)
    received = lax.ppermute(to_core, "marker", OTHER_CORE)
    kept, panel, ahead = projection(blocks, AHEAD, 1, genotypes, panel, ahead, (to_core,))
    to_chip = kept + received
    from_chip = lax.ppermute(to_chip, "marker", OTHER_CHIP)
    to_core, panel, ahead = projection(blocks, AHEAD, 2, genotypes, panel, ahead, (to_chip,))
    from_core = lax.ppermute(to_core, "marker", OTHER_CORE)
    kept, panel, ahead = projection(blocks, AHEAD, 3, genotypes, panel, ahead, (to_core,))
    with jax.named_scope("features"):
        features = pl.pallas_call(
            features_kernel,
            out_shape=jax.ShapeDtypeStruct((quarter, feats), jnp.bfloat16),
            in_specs=[vmem()] * 3,
            out_specs=vmem(),
            compiler_params=small,
        )(kept + from_chip, from_core, phases.reshape(1, feats))
    features_other = lax.ppermute(features, "marker", OTHER_CORE)

    height = feats // groups
    piece = (2 * height + height // 2, LANES)

    def gram_of(from_other_core, out_shape, *operands):
        return pl.pallas_call(
            functools.partial(gram_kernel, from_other_core),
            out_shape=out_shape,
            in_specs=[vmem()] * len(operands),
            out_specs=vmem(),
            compiler_params=small,
            cost_estimate=pl.CostEstimate(flops=feats * quarter * (feats + 2 * LANES), bytes_accessed=0, transcendentals=0),
        )(*operands)

    with jax.named_scope("gram_cross"):
        twice = jnp.concatenate([phenotypes, phenotypes], axis=1)
        partial_sums = gram_of(False, jax.ShapeDtypeStruct((feats, feats // 2 + LANES), jnp.float32), features, twice)
        partial_sums = gram_of(
            True, jax.ShapeDtypeStruct((groups,) + piece, jnp.bfloat16), features_other, twice, partial_sums
        )
    pieces = lax.all_to_all(partial_sums, "animal", 0, 0)
    with jax.named_scope("sum_animals"):
        own = pl.pallas_call(
            sum_kernel,
            out_shape=jax.ShapeDtypeStruct(piece, jnp.float32),
            in_specs=[vmem()],
            out_specs=vmem(),
            compiler_params=small,
        )(pieces)
    other = lax.ppermute(own, "marker", OTHER_CORE)
    with jax.named_scope("join_cores"):
        here = pl.pallas_call(
            join_kernel,
            out_shape=jax.ShapeDtypeStruct((2,) + own.shape, jnp.float32),
            in_specs=[vmem()] * 2,
            out_specs=vmem(),
            compiler_params=small,
        )(own, other)
    there = lax.ppermute(here, "marker", OTHER_CHIP)
    with jax.named_scope("finish"):
        return pl.pallas_call(
            functools.partial(finish_kernel, animals_all),
            out_shape=(
                jax.ShapeDtypeStruct((feats // groups, feats), jnp.float32),
                jax.ShapeDtypeStruct((feats // groups, traits), jnp.float32),
            ),
            in_specs=[vmem()] * 2,
            out_specs=(vmem(), vmem()),
            compiler_params=small,
        )(here, there)


def solution(mesh):
    in_specs = (P("animal", "marker"), P("marker", None), P(), P("animal", None))
    out_specs = (P("animal", None), P("animal", None))
    return jax.shard_map(
        on_device, mesh=mesh, in_specs=in_specs, out_specs=out_specs, check_vma=False
    )
```

```python
import functools
import math

import jax
import jax.numpy as jnp
from jax import lax
from jax.experimental import pallas as pl
from jax.experimental.pallas import tpu as pltpu
from jax.sharding import PartitionSpec as P

OTHER_CORE = [(0, 1), (1, 0), (2, 3), (3, 2)]
OTHER_CHIP = [(0, 2), (2, 0), (1, 3), (3, 1)]
TILE = 256
LANES = 128
PARTS = [(0, 1024), (1024, 1024), (2048, 2048), (4096, 2048), (6144, 1536), (7680, 512)]
AHEAD = (0, 4, 2, 3)
SINE = (-8.88576566829991, 58.46592923637672, -115.4012466635561, 108.25774031408996, -55.913345915340486)


def to_turns(radians):
    steps = jnp.round(radians * (65536.0 / (2.0 * math.pi))).astype(jnp.int32)
    return ((steps << 16) >> 16).astype(jnp.int16)


def copies(geno_hbm, first, geno, sem, parts):
    rows = geno.shape[0]
    return {
        step: pltpu.make_async_copy(
            geno_hbm.at[pl.ds(pl.multiple_of(first, 32), rows), pl.ds(PARTS[step][0], PARTS[step][1])],
            geno.at[:, pl.ds(PARTS[step][0], PARTS[step][1])],
            sem.at[step],
        )
        for step in parts
    }


def row_of(block):
    place = lax.axis_index("marker")
    chip, core = place // 2, place % 2
    other_chip, other_core, quarter_rows, offset, _ = block
    chip = 1 - chip if other_chip else chip
    core = 1 - core if other_core else core
    return (chip * 2 + core) * quarter_rows + offset


def projection_kernel(block, came_parts, next_block, next_parts, loads_panel, *refs):
    refs = list(refs)
    geno_hbm, panel_in = refs.pop(0), refs.pop(0)
    came_ref = refs.pop(0) if came_parts else None
    if not loads_panel:
        refs.pop(0)
    out_ref = refs.pop(0)
    panel_ref = refs.pop(0) if loads_panel else panel_in
    ahead_ref = refs.pop(0) if next_parts else None
    geno, geno_sem, ahead_sem, panel_sem = refs
    came_cols = PARTS[came_parts][0]
    geno_copies = copies(geno_hbm, row_of(block), geno, geno_sem, range(came_parts, len(PARTS)))
    panel_copies = []
    if loads_panel:
        panel_copies = [
            pltpu.make_async_copy(panel_in.at[pl.ds(start, width)], panel_ref.at[pl.ds(start, width)], panel_sem.at[step])
            for step, (start, width) in enumerate(PARTS)
        ]
    ahead_copies = copies(geno_hbm, row_of(next_block), ahead_ref, ahead_sem, range(next_parts)) if next_parts else {}
    for step in range(len(PARTS)):
        if loads_panel:
            panel_copies[step].start()
        if step >= came_parts:
            geno_copies[step].start()
    def start_ahead():
        for copy in ahead_copies.values():
            copy.start()

    late = 1 if came_parts == 2 else None
    if late is None:
        start_ahead()

    def run(*sums):
        for step, (start, width) in enumerate(PARTS):
            if loads_panel:
                panel_copies[step].wait()
            if step >= came_parts:
                geno_copies[step].wait()
            if step == late:
                start_ahead()
            for tile in range(start, start + width, TILE):
                source = came_ref if tile < came_cols else geno
                dosage = (source[:, tile : tile + TILE] - 1).astype(jnp.float32).astype(jnp.bfloat16)
                slot = tile // TILE % 2
                for unit in range(2):
                    pltpu.matmul_push_rhs(panel_ref[tile : tile + TILE, unit * TILE : (unit + 1) * TILE], slot, unit)
                for unit in range(2):
                    pltpu.matmul_acc_lhs(sums[unit], dosage, slot)
        for unit in range(2):
            out_ref[:, unit * TILE : (unit + 1) * TILE] = to_turns(pltpu.matmul_pop(sums[unit]))

    pl.run_scoped(run, *[pltpu.ACC(unit)((geno.shape[0], TILE), jnp.float32) for unit in range(2)])
    for copy in ahead_copies.values():
        copy.wait()


def projection(blocks, ahead, step, geno, panel, came, after=()):
    block, loads_panel = blocks[step], step == 0
    last = step == len(blocks) - 1
    rows, markers, feats = block[-1], geno.shape[1], panel.shape[1]
    next_parts = 0 if last else ahead[step + 1]
    outs = [jax.ShapeDtypeStruct((rows, feats), jnp.int16)]
    if loads_panel:
        outs.append(pltpu.VMEM((markers, feats), jnp.bfloat16))
    if next_parts:
        outs.append(pltpu.VMEM((blocks[step + 1][-1], PARTS[next_parts][0]), jnp.int32))
    operands = [geno, panel] + ([came] if ahead[step] else []) + list(after)
    sems = pltpu.SemaphoreType.DMA((len(PARTS),))
    scratch = rows * markers * 4
    with jax.named_scope(f"projection_block_{step}"):
        made = pl.pallas_call(
            functools.partial(projection_kernel, block, ahead[step], None if last else blocks[step + 1], next_parts, loads_panel),
            out_shape=tuple(outs),
            in_specs=[anywhere(), anywhere() if loads_panel else vmem()] + [vmem()] * bool(ahead[step]) + [anywhere()] * len(after),
            out_specs=(vmem(),) * len(outs),
            scratch_shapes=[pltpu.VMEM((rows, markers), jnp.int32), sems, sems, sems],
            compiler_params=pltpu.CompilerParams(vmem_limit_bytes=scratch + 6 * 2**20),
            cost_estimate=pl.CostEstimate(
                flops=2 * rows * markers * feats, bytes_accessed=scratch + loads_panel * markers * feats * 2, transcendentals=0
            ),
        )(*operands)
    made = list(made)
    return made[0], made[1] if loads_panel else panel, made[-1] if next_parts else None


def features_kernel(kept_ref, core_ref, phase_ref, out_ref):
    phase = jnp.round(phase_ref[...] * (2.0**32 / (2.0 * math.pi))).astype(jnp.int32)
    turns = ((kept_ref[...].astype(jnp.int32) + core_ref[...].astype(jnp.int32)) << 16) + phase
    t = jnp.abs(turns.astype(jnp.float32) * 2.0**-32) - 0.25
    square = t * t
    value = jnp.full_like(t, SINE[-1])
    for factor in SINE[-2::-1]:
        value = value * square + factor
    out_ref[...] = (value * t).astype(jnp.bfloat16)


def gram_kernel(from_other_core, feature_ref, pheno_ref, *refs):
    out_ref = refs[-1]
    rows, feats = feature_ref.shape
    half = feats // 2
    place = lax.axis_index("marker")
    core = place % 2
    spot = place + 1 - 2 * core if from_other_core else place
    features = feature_ref[...]
    phenotypes = pheno_ref[pl.ds(pl.multiple_of(spot * rows, rows), rows)]

    def product(right):
        return lax.dot_general(features, right, (((0,), (0,)), ((), ())), preferred_element_type=jnp.float32)

    gram = product(feature_ref[:, pl.ds(pl.multiple_of(core * half, half), half)])
    cross = product(phenotypes)
    if not from_other_core:
        out_ref[:, :half] = gram
        out_ref[:, half:] = cross
        return
    pieces = out_ref.shape[0]
    height = feats // pieces
    gram = (gram + refs[0][:, :half]).astype(jnp.bfloat16)
    cross = (cross + refs[0][:, half:]).reshape(pieces, 2, height // 2, LANES)
    left = lax.broadcasted_iota(jnp.int32, (pieces, height // 2, LANES), 2) < LANES // 2
    cross = jnp.where(left, cross[:, 0], cross[:, 1])
    high = cross.astype(jnp.bfloat16)
    low = (cross - high.astype(jnp.float32)).astype(jnp.bfloat16)
    halves = [gram[:, start : start + LANES].reshape(pieces, height, LANES) for start in (0, LANES)]
    out_ref[...] = jnp.concatenate(halves + [jnp.where(core == 0, high, low)], axis=1)


def sum_kernel(in_ref, out_ref):
    out_ref[...] = jnp.sum(in_ref[...].astype(jnp.float32), axis=0)


def join_kernel(own_ref, other_ref, out_ref):
    core = lax.axis_index("marker") % 2
    out_ref[core] = own_ref[...]
    out_ref[1 - core] = other_ref[...]


def finish_kernel(animals_all, here_ref, there_ref, gram_ref, cross_ref):
    height = gram_ref.shape[0]
    total = here_ref[...] + there_ref[...]
    for core in range(2):
        for part in range(2):
            start = (2 * core + part) * LANES
            gram_ref[:, start : start + LANES] = total[core, part * height : (part + 1) * height] / animals_all
    cross = (total[0, 2 * height :] + total[1, 2 * height :]) / math.sqrt(animals_all)
    cross_ref[: height // 2] = cross[:, : LANES // 2]
    cross_ref[height // 2 :] = cross[:, LANES // 2 :]


def vmem():
    return pl.BlockSpec(memory_space=pltpu.VMEM)


def anywhere():
    return pl.BlockSpec(memory_space=pl.ANY)


def on_device(genotypes, frequencies, phases, phenotypes):
    rows, markers = genotypes.shape
    feats = frequencies.shape[1]
    traits = phenotypes.shape[1]
    groups = lax.axis_size("animal")
    animals_all = float(groups * rows)
    quarter = rows // 4
    small = pltpu.CompilerParams(vmem_limit_bytes=12 * 2**20)
    genotypes = pltpu.with_memory_space_constraint(genotypes, pltpu.HBM)
    frequencies = pltpu.with_memory_space_constraint(frequencies, pltpu.HBM)

    blocks = [(True, True, quarter, 0, quarter), (True, False, quarter, 0, quarter), (False, True, quarter, 0, quarter), (False, False, quarter, 0, quarter)]
    to_core, panel, ahead = projection(blocks, AHEAD, 0, genotypes, frequencies, None)
    received = lax.ppermute(to_core, "marker", OTHER_CORE)
    kept, panel, ahead = projection(blocks, AHEAD, 1, genotypes, panel, ahead, (to_core,))
    to_chip = kept + received
    from_chip = lax.ppermute(to_chip, "marker", OTHER_CHIP)
    to_core, panel, ahead = projection(blocks, AHEAD, 2, genotypes, panel, ahead, (to_chip,))
    from_core = lax.ppermute(to_core, "marker", OTHER_CORE)
    kept, panel, ahead = projection(blocks, AHEAD, 3, genotypes, panel, ahead, (to_core,))
    with jax.named_scope("features"):
        features = pl.pallas_call(
            features_kernel,
            out_shape=jax.ShapeDtypeStruct((quarter, feats), jnp.bfloat16),
            in_specs=[vmem()] * 3,
            out_specs=vmem(),
            compiler_params=small,
        )(kept + from_chip, from_core, phases.reshape(1, feats))
    features_other = lax.ppermute(features, "marker", OTHER_CORE)

    height = feats // groups
    piece = (2 * height + height // 2, LANES)

    def gram_of(from_other_core, out_shape, *operands):
        return pl.pallas_call(
            functools.partial(gram_kernel, from_other_core),
            out_shape=out_shape,
            in_specs=[vmem()] * len(operands),
            out_specs=vmem(),
            compiler_params=small,
            cost_estimate=pl.CostEstimate(flops=feats * quarter * (feats + 2 * LANES), bytes_accessed=0, transcendentals=0),
        )(*operands)

    with jax.named_scope("gram_cross"):
        twice = jnp.concatenate([phenotypes, phenotypes], axis=1)
        partial_sums = gram_of(False, jax.ShapeDtypeStruct((feats, feats // 2 + LANES), jnp.float32), features, twice)
        partial_sums = gram_of(
            True, jax.ShapeDtypeStruct((groups,) + piece, jnp.bfloat16), features_other, twice, partial_sums
        )
    pieces = lax.all_to_all(partial_sums, "animal", 0, 0)
    with jax.named_scope("sum_animals"):
        own = pl.pallas_call(
            sum_kernel,
            out_shape=jax.ShapeDtypeStruct(piece, jnp.float32),
            in_specs=[vmem()],
            out_specs=vmem(),
            compiler_params=small,
        )(pieces)
    other = lax.ppermute(own, "marker", OTHER_CORE)
    with jax.named_scope("join_cores"):
        here = pl.pallas_call(
            join_kernel,
            out_shape=jax.ShapeDtypeStruct((2,) + own.shape, jnp.float32),
            in_specs=[vmem()] * 2,
            out_specs=vmem(),
            compiler_params=small,
        )(own, other)
    there = lax.ppermute(here, "marker", OTHER_CHIP)
    with jax.named_scope("finish"):
        return pl.pallas_call(
            functools.partial(finish_kernel, animals_all),
            out_shape=(
                jax.ShapeDtypeStruct((feats // groups, feats), jnp.float32),
                jax.ShapeDtypeStruct((feats // groups, traits), jnp.float32),
            ),
            in_specs=[vmem()] * 2,
            out_specs=(vmem(), vmem()),
            compiler_params=small,
        )(here, there)


def solution(mesh):
    in_specs = (P("animal", "marker"), P("marker", None), P(), P("animal", None))
    out_specs = (P("animal", None), P("animal", None))
    return jax.shard_map(
        on_device, mesh=mesh, in_specs=in_specs, out_specs=out_specs, check_vma=False
    )
```

```python
import functools
import math

import jax
import jax.numpy as jnp
from jax import lax
from jax.experimental import pallas as pl
from jax.experimental.pallas import tpu as pltpu
from jax.sharding import PartitionSpec as P

OTHER_CORE = [(0, 1), (1, 0), (2, 3), (3, 2)]
OTHER_CHIP = [(0, 2), (2, 0), (1, 3), (3, 1)]
TILE = 256
LANES = 128
PARTS = [(0, 1024), (1024, 1024), (2048, 2048), (4096, 2048), (6144, 1536), (7680, 512)]
AHEAD = (0, 4, 2, 3)
SINE = (-8.88576566829991, 58.46592923637672, -115.4012466635561, 108.25774031408996, -55.913345915340486)


def to_turns(radians):
    steps = jnp.round(radians * (65536.0 / (2.0 * math.pi))).astype(jnp.int32)
    return ((steps << 16) >> 16).astype(jnp.int16)


def copies(geno_hbm, first, geno, sem, parts):
    rows = geno.shape[0]
    return {
        step: pltpu.make_async_copy(
            geno_hbm.at[pl.ds(pl.multiple_of(first, 32), rows), pl.ds(PARTS[step][0], PARTS[step][1])],
            geno.at[:, pl.ds(PARTS[step][0], PARTS[step][1])],
            sem.at[step],
        )
        for step in parts
    }


def row_of(block):
    place = lax.axis_index("marker")
    chip, core = place // 2, place % 2
    other_chip, other_core, quarter_rows, offset, _ = block
    chip = 1 - chip if other_chip else chip
    core = 1 - core if other_core else core
    return (chip * 2 + core) * quarter_rows + offset


def projection_kernel(block, came_parts, next_block, next_parts, loads_panel, *refs):
    refs = list(refs)
    geno_hbm, panel_in = refs.pop(0), refs.pop(0)
    came_ref = refs.pop(0) if came_parts else None
    if not loads_panel:
        refs.pop(0)
    out_ref = refs.pop(0)
    panel_ref = refs.pop(0) if loads_panel else panel_in
    ahead_ref = refs.pop(0) if next_parts else None
    geno, geno_sem, ahead_sem, panel_sem = refs
    came_cols = PARTS[came_parts][0]
    geno_copies = copies(geno_hbm, row_of(block), geno, geno_sem, range(came_parts, len(PARTS)))
    panel_copies = []
    if loads_panel:
        panel_copies = [
            pltpu.make_async_copy(panel_in.at[pl.ds(start, width)], panel_ref.at[pl.ds(start, width)], panel_sem.at[step])
            for step, (start, width) in enumerate(PARTS)
        ]
    ahead_copies = copies(geno_hbm, row_of(next_block), ahead_ref, ahead_sem, range(next_parts)) if next_parts else {}
    for step in range(len(PARTS)):
        if loads_panel:
            panel_copies[step].start()
        if step >= came_parts:
            geno_copies[step].start()
    def start_ahead():
        for copy in ahead_copies.values():
            copy.start()

    late = 1 if came_parts == 2 else None
    if late is None:
        start_ahead()

    def run(*sums):
        for step, (start, width) in enumerate(PARTS):
            if loads_panel:
                panel_copies[step].wait()
            if step >= came_parts:
                geno_copies[step].wait()
            if step == late:
                start_ahead()
            for tile in range(start, start + width, TILE):
                source = came_ref if tile < came_cols else geno
                dosage = (source[:, tile : tile + TILE] - 1).astype(jnp.float32).astype(jnp.bfloat16)
                slot = tile // TILE % 2
                for unit in range(2):
                    pltpu.matmul_push_rhs(panel_ref[tile : tile + TILE, unit * TILE : (unit + 1) * TILE], slot, unit)
                for unit in range(2):
                    pltpu.matmul_acc_lhs(sums[unit], dosage, slot)
        for unit in range(2):
            out_ref[:, unit * TILE : (unit + 1) * TILE] = to_turns(pltpu.matmul_pop(sums[unit]))

    pl.run_scoped(run, *[pltpu.ACC(unit)((geno.shape[0], TILE), jnp.float32) for unit in range(2)])
    for copy in ahead_copies.values():
        copy.wait()


def projection(blocks, ahead, step, geno, panel, came, after=()):
    block, loads_panel = blocks[step], step == 0
    last = step == len(blocks) - 1
    rows, markers, feats = block[-1], geno.shape[1], panel.shape[1]
    next_parts = 0 if last else ahead[step + 1]
    outs = [jax.ShapeDtypeStruct((rows, feats), jnp.int16)]
    if loads_panel:
        outs.append(pltpu.VMEM((markers, feats), jnp.bfloat16))
    if next_parts:
        outs.append(pltpu.VMEM((blocks[step + 1][-1], PARTS[next_parts][0]), jnp.int32))
    operands = [geno, panel] + ([came] if ahead[step] else []) + list(after)
    sems = pltpu.SemaphoreType.DMA((len(PARTS),))
    scratch = rows * markers * 4
    with jax.named_scope(f"projection_block_{step}"):
        made = pl.pallas_call(
            functools.partial(projection_kernel, block, ahead[step], None if last else blocks[step + 1], next_parts, loads_panel),
            out_shape=tuple(outs),
            in_specs=[anywhere(), anywhere() if loads_panel else vmem()] + [vmem()] * bool(ahead[step]) + [anywhere()] * len(after),
            out_specs=(vmem(),) * len(outs),
            scratch_shapes=[pltpu.VMEM((rows, markers), jnp.int32), sems, sems, sems],
            compiler_params=pltpu.CompilerParams(vmem_limit_bytes=scratch + 6 * 2**20),
            cost_estimate=pl.CostEstimate(
                flops=2 * rows * markers * feats, bytes_accessed=scratch + loads_panel * markers * feats * 2, transcendentals=0
            ),
        )(*operands)
    made = list(made)
    return made[0], made[1] if loads_panel else panel, made[-1] if next_parts else None


def features_kernel(kept_ref, core_ref, phase_ref, out_ref):
    phase = jnp.round(phase_ref[...] * (2.0**32 / (2.0 * math.pi))).astype(jnp.int32)
    turns = ((kept_ref[...].astype(jnp.int32) + core_ref[...].astype(jnp.int32)) << 16) + phase
    t = jnp.abs(turns.astype(jnp.float32) * 2.0**-32) - 0.25
    square = t * t
    value = jnp.full_like(t, SINE[-1])
    for factor in SINE[-2::-1]:
        value = value * square + factor
    out_ref[...] = (value * t).astype(jnp.bfloat16)


def gram_kernel(from_other_core, feature_ref, pheno_ref, *refs):
    out_ref = refs[-1]
    rows, feats = feature_ref.shape
    half = feats // 2
    place = lax.axis_index("marker")
    core = place % 2
    spot = place + 1 - 2 * core if from_other_core else place
    features = feature_ref[...]
    phenotypes = pheno_ref[pl.ds(pl.multiple_of(spot * rows, rows), rows)]

    def product(right):
        return lax.dot_general(features, right, (((0,), (0,)), ((), ())), preferred_element_type=jnp.float32)

    gram = product(feature_ref[:, pl.ds(pl.multiple_of(core * half, half), half)])
    cross = product(phenotypes)
    if not from_other_core:
        out_ref[:, :half] = gram
        out_ref[:, half:] = cross
        return
    pieces = out_ref.shape[0]
    height = feats // pieces
    gram = (gram + refs[0][:, :half]).astype(jnp.bfloat16)
    cross = (cross + refs[0][:, half:]).reshape(pieces, 2, height // 2, LANES)
    left = lax.broadcasted_iota(jnp.int32, (pieces, height // 2, LANES), 2) < LANES // 2
    cross = jnp.where(left, cross[:, 0], cross[:, 1])
    high = cross.astype(jnp.bfloat16)
    low = (cross - high.astype(jnp.float32)).astype(jnp.bfloat16)
    halves = [gram[:, start : start + LANES].reshape(pieces, height, LANES) for start in (0, LANES)]
    out_ref[...] = jnp.concatenate(halves + [jnp.where(core == 0, high, low)], axis=1)


def sum_kernel(in_ref, out_ref):
    out_ref[...] = jnp.sum(in_ref[...].astype(jnp.float32), axis=0)


def join_kernel(own_ref, other_ref, out_ref):
    core = lax.axis_index("marker") % 2
    cross = out_ref.shape[0] - own_ref.shape[0]
    out_ref[pl.ds(pl.multiple_of(core * cross, cross), cross)] = own_ref[:cross]
    out_ref[pl.ds(pl.multiple_of((1 - core) * cross, cross), cross)] = other_ref[:cross]
    out_ref[2 * cross :] = own_ref[cross:] + other_ref[cross:]


def finish_kernel(animals_all, here_ref, there_ref, gram_ref, cross_ref):
    height = gram_ref.shape[0]
    for part in range(4):
        rows = slice(part * height, (part + 1) * height)
        gram_ref[:, part * LANES : (part + 1) * LANES] = (here_ref[rows] + there_ref[rows]) / animals_all
    cross = (here_ref[4 * height :] + there_ref[4 * height :]) / math.sqrt(animals_all)
    cross_ref[: height // 2] = cross[:, : LANES // 2]
    cross_ref[height // 2 :] = cross[:, LANES // 2 :]


def vmem():
    return pl.BlockSpec(memory_space=pltpu.VMEM)


def anywhere():
    return pl.BlockSpec(memory_space=pl.ANY)


def on_device(genotypes, frequencies, phases, phenotypes):
    rows, markers = genotypes.shape
    feats = frequencies.shape[1]
    traits = phenotypes.shape[1]
    groups = lax.axis_size("animal")
    animals_all = float(groups * rows)
    quarter = rows // 4
    small = pltpu.CompilerParams(vmem_limit_bytes=12 * 2**20)
    genotypes = pltpu.with_memory_space_constraint(genotypes, pltpu.HBM)
    frequencies = pltpu.with_memory_space_constraint(frequencies, pltpu.HBM)

    blocks = [(True, True, quarter, 0, quarter), (True, False, quarter, 0, quarter), (False, True, quarter, 0, quarter), (False, False, quarter, 0, quarter)]
    to_core, panel, ahead = projection(blocks, AHEAD, 0, genotypes, frequencies, None)
    received = lax.ppermute(to_core, "marker", OTHER_CORE)
    kept, panel, ahead = projection(blocks, AHEAD, 1, genotypes, panel, ahead, (to_core,))
    to_chip = kept + received
    from_chip = lax.ppermute(to_chip, "marker", OTHER_CHIP)
    to_core, panel, ahead = projection(blocks, AHEAD, 2, genotypes, panel, ahead, (to_chip,))
    from_core = lax.ppermute(to_core, "marker", OTHER_CORE)
    kept, panel, ahead = projection(blocks, AHEAD, 3, genotypes, panel, ahead, (to_core,))
    with jax.named_scope("features"):
        features = pl.pallas_call(
            features_kernel,
            out_shape=jax.ShapeDtypeStruct((quarter, feats), jnp.bfloat16),
            in_specs=[vmem()] * 3,
            out_specs=vmem(),
            compiler_params=small,
        )(kept + from_chip, from_core, phases.reshape(1, feats))
    features_other = lax.ppermute(features, "marker", OTHER_CORE)

    height = feats // groups
    piece = (2 * height + height // 2, LANES)

    def gram_of(from_other_core, out_shape, *operands):
        return pl.pallas_call(
            functools.partial(gram_kernel, from_other_core),
            out_shape=out_shape,
            in_specs=[vmem()] * len(operands),
            out_specs=vmem(),
            compiler_params=small,
            cost_estimate=pl.CostEstimate(flops=feats * quarter * (feats + 2 * LANES), bytes_accessed=0, transcendentals=0),
        )(*operands)

    with jax.named_scope("gram_cross"):
        twice = jnp.concatenate([phenotypes, phenotypes], axis=1)
        partial_sums = gram_of(False, jax.ShapeDtypeStruct((feats, feats // 2 + LANES), jnp.float32), features, twice)
        partial_sums = gram_of(
            True, jax.ShapeDtypeStruct((groups,) + piece, jnp.bfloat16), features_other, twice, partial_sums
        )
    pieces = lax.all_to_all(partial_sums, "animal", 0, 0)
    with jax.named_scope("sum_animals"):
        own = pl.pallas_call(
            sum_kernel,
            out_shape=jax.ShapeDtypeStruct(piece, jnp.float32),
            in_specs=[vmem()],
            out_specs=vmem(),
            compiler_params=small,
        )(pieces)
    other = lax.ppermute(own, "marker", OTHER_CORE)
    with jax.named_scope("join_cores"):
        here = pl.pallas_call(
            join_kernel,
            out_shape=jax.ShapeDtypeStruct((own.shape[0] + 2 * height, LANES), jnp.float32),
            in_specs=[vmem()] * 2,
            out_specs=vmem(),
            compiler_params=small,
        )(own, other)
    there = lax.ppermute(here, "marker", OTHER_CHIP)
    with jax.named_scope("finish"):
        return pl.pallas_call(
            functools.partial(finish_kernel, animals_all),
            out_shape=(
                jax.ShapeDtypeStruct((feats // groups, feats), jnp.float32),
                jax.ShapeDtypeStruct((feats // groups, traits), jnp.float32),
            ),
            in_specs=[vmem()] * 2,
            out_specs=(vmem(), vmem()),
            compiler_params=small,
        )(here, there)


def solution(mesh):
    in_specs = (P("animal", "marker"), P("marker", None), P(), P("animal", None))
    out_specs = (P("animal", None), P("animal", None))
    return jax.shard_map(
        on_device, mesh=mesh, in_specs=in_specs, out_specs=out_specs, check_vma=False
    )
```

```python
import functools
import math

import jax
import jax.numpy as jnp
from jax import lax
from jax.experimental import pallas as pl
from jax.experimental.pallas import tpu as pltpu
from jax.sharding import PartitionSpec as P

OTHER_CORE = [(0, 1), (1, 0), (2, 3), (3, 2)]
OTHER_CHIP = [(0, 2), (2, 0), (1, 3), (3, 1)]
TILE = 256
LANES = 128
PARTS = [(0, 1024), (1024, 1024), (2048, 2048), (4096, 2048), (6144, 1536), (7680, 512)]
AHEAD = (0, 4, 2, 3)
SINE = (-8.88576566829991, 58.46592923637672, -115.4012466635561, 108.25774031408996, -55.913345915340486)


def to_turns(radians):
    steps = jnp.round(radians * (65536.0 / (2.0 * math.pi))).astype(jnp.int32)
    return ((steps << 16) >> 16).astype(jnp.int16)


def copies(geno_hbm, first, geno, sem, parts):
    rows = geno.shape[0]
    return {
        step: pltpu.make_async_copy(
            geno_hbm.at[pl.ds(pl.multiple_of(first, 32), rows), pl.ds(PARTS[step][0], PARTS[step][1])],
            geno.at[:, pl.ds(PARTS[step][0], PARTS[step][1])],
            sem.at[step],
        )
        for step in parts
    }


def row_of(block):
    place = lax.axis_index("marker")
    chip, core = place // 2, place % 2
    other_chip, other_core, quarter_rows, offset, _ = block
    chip = 1 - chip if other_chip else chip
    core = 1 - core if other_core else core
    return (chip * 2 + core) * quarter_rows + offset


def projection_kernel(block, came_parts, next_block, next_parts, loads_panel, *refs):
    refs = list(refs)
    geno_hbm, panel_in = refs.pop(0), refs.pop(0)
    came_ref = refs.pop(0) if came_parts else None
    if not loads_panel:
        refs.pop(0)
    out_ref = refs.pop(0)
    panel_ref = refs.pop(0) if loads_panel else panel_in
    ahead_ref = refs.pop(0) if next_parts else None
    geno, geno_sem, ahead_sem, panel_sem = refs
    came_cols = PARTS[came_parts][0]
    geno_copies = copies(geno_hbm, row_of(block), geno, geno_sem, range(came_parts, len(PARTS)))
    panel_copies = []
    if loads_panel:
        panel_copies = [
            pltpu.make_async_copy(panel_in.at[pl.ds(start, width)], panel_ref.at[pl.ds(start, width)], panel_sem.at[step])
            for step, (start, width) in enumerate(PARTS)
        ]
    ahead_copies = copies(geno_hbm, row_of(next_block), ahead_ref, ahead_sem, range(next_parts)) if next_parts else {}
    for step in range(len(PARTS)):
        if loads_panel:
            panel_copies[step].start()
        if step >= came_parts:
            geno_copies[step].start()
    def start_ahead():
        for copy in ahead_copies.values():
            copy.start()

    late = 1 if came_parts == 2 else None
    if late is None:
        start_ahead()

    def run(*sums):
        for step, (start, width) in enumerate(PARTS):
            if loads_panel:
                panel_copies[step].wait()
            if step >= came_parts:
                geno_copies[step].wait()
            if step == late:
                start_ahead()
            for tile in range(start, start + width, TILE):
                source = came_ref if tile < came_cols else geno
                dosage = (source[:, tile : tile + TILE] - 1).astype(jnp.float32).astype(jnp.bfloat16)
                slot = tile // TILE % 2
                for unit in range(2):
                    pltpu.matmul_push_rhs(panel_ref[tile : tile + TILE, unit * TILE : (unit + 1) * TILE], slot, unit)
                for unit in range(2):
                    pltpu.matmul_acc_lhs(sums[unit], dosage, slot)
        for unit in range(2):
            out_ref[:, unit * TILE : (unit + 1) * TILE] = to_turns(pltpu.matmul_pop(sums[unit]))

    pl.run_scoped(run, *[pltpu.ACC(unit)((geno.shape[0], TILE), jnp.float32) for unit in range(2)])
    for copy in ahead_copies.values():
        copy.wait()


def projection(blocks, ahead, step, geno, panel, came, after=()):
    block, loads_panel = blocks[step], step == 0
    last = step == len(blocks) - 1
    rows, markers, feats = block[-1], geno.shape[1], panel.shape[1]
    next_parts = 0 if last else ahead[step + 1]
    outs = [jax.ShapeDtypeStruct((rows, feats), jnp.int16)]
    if loads_panel:
        outs.append(pltpu.VMEM((markers, feats), jnp.bfloat16))
    if next_parts:
        outs.append(pltpu.VMEM((blocks[step + 1][-1], PARTS[next_parts][0]), jnp.int32))
    operands = [geno, panel] + ([came] if ahead[step] else []) + list(after)
    sems = pltpu.SemaphoreType.DMA((len(PARTS),))
    scratch = rows * markers * 4
    with jax.named_scope(f"projection_block_{step}"):
        made = pl.pallas_call(
            functools.partial(projection_kernel, block, ahead[step], None if last else blocks[step + 1], next_parts, loads_panel),
            out_shape=tuple(outs),
            in_specs=[anywhere(), anywhere() if loads_panel else vmem()] + [vmem()] * bool(ahead[step]) + [anywhere()] * len(after),
            out_specs=(vmem(),) * len(outs),
            scratch_shapes=[pltpu.VMEM((rows, markers), jnp.int32), sems, sems, sems],
            compiler_params=pltpu.CompilerParams(vmem_limit_bytes=scratch + 6 * 2**20),
            cost_estimate=pl.CostEstimate(
                flops=2 * rows * markers * feats, bytes_accessed=scratch + loads_panel * markers * feats * 2, transcendentals=0
            ),
        )(*operands)
    made = list(made)
    return made[0], made[1] if loads_panel else panel, made[-1] if next_parts else None


def features_kernel(kept_ref, core_ref, phase_ref, out_ref):
    phase = jnp.round(phase_ref[...] * (2.0**32 / (2.0 * math.pi))).astype(jnp.int32)
    turns = ((kept_ref[...].astype(jnp.int32) + core_ref[...].astype(jnp.int32)) << 16) + phase
    t = jnp.abs(turns.astype(jnp.float32) * 2.0**-32) - 0.25
    square = t * t
    value = jnp.full_like(t, SINE[-1])
    for factor in SINE[-2::-1]:
        value = value * square + factor
    out_ref[...] = (value * t).astype(jnp.bfloat16)


def gram_kernel(from_other_core, feature_ref, pheno_ref, *refs):
    out_ref = refs[-1]
    rows, feats = feature_ref.shape
    half = feats // 2
    place = lax.axis_index("marker")
    core = place % 2
    spot = place + 1 - 2 * core if from_other_core else place
    features = feature_ref[...]
    phenotypes = pheno_ref[pl.ds(pl.multiple_of(spot * rows, rows), rows)]

    def product(right):
        return lax.dot_general(features, right, (((0,), (0,)), ((), ())), preferred_element_type=jnp.float32)

    gram = product(feature_ref[:, pl.ds(pl.multiple_of(core * half, half), half)])
    cross = product(phenotypes)
    if not from_other_core:
        out_ref[:, :half] = gram
        out_ref[:, half:] = cross
        return
    pieces = out_ref.shape[0]
    height = feats // pieces
    gram = (gram + refs[0][:, :half]).astype(jnp.bfloat16)
    cross = (cross + refs[0][:, half:]).reshape(pieces, 2, height // 2, LANES)
    left = lax.broadcasted_iota(jnp.int32, (pieces, height // 2, LANES), 2) < LANES // 2
    cross = jnp.where(left, cross[:, 0], cross[:, 1])
    high = cross.astype(jnp.bfloat16)
    low = (cross - high.astype(jnp.float32)).astype(jnp.bfloat16)
    halves = [gram[:, start : start + LANES].reshape(pieces, height, LANES) for start in (0, LANES)]
    out_ref[...] = jnp.concatenate(halves + [jnp.where(core == 0, high, low)], axis=1)


def sum_kernel(in_ref, out_ref):
    out_ref[...] = jnp.sum(in_ref[...].astype(jnp.float32), axis=0)


def join_kernel(own_ref, other_ref, out_ref):
    core = lax.axis_index("marker") % 2
    cross = out_ref.shape[0] - own_ref.shape[0]
    out_ref[pl.ds(pl.multiple_of(core * cross, cross), cross)] = own_ref[:cross]
    out_ref[pl.ds(pl.multiple_of((1 - core) * cross, cross), cross)] = other_ref[:cross]
    out_ref[2 * cross :] = own_ref[cross:] + other_ref[cross:]


def finish_kernel(animals_all, here_ref, there_ref, gram_ref, cross_ref):
    height = gram_ref.shape[0]
    for part in range(4):
        rows = slice(part * height, (part + 1) * height)
        gram_ref[:, part * LANES : (part + 1) * LANES] = (here_ref[rows] + there_ref[rows]) * (1.0 / animals_all)
    cross = (here_ref[4 * height :] + there_ref[4 * height :]) * (1.0 / math.sqrt(animals_all))
    cross_ref[: height // 2] = cross[:, : LANES // 2]
    cross_ref[height // 2 :] = cross[:, LANES // 2 :]


def vmem():
    return pl.BlockSpec(memory_space=pltpu.VMEM)


def anywhere():
    return pl.BlockSpec(memory_space=pl.ANY)


def on_device(genotypes, frequencies, phases, phenotypes):
    rows, markers = genotypes.shape
    feats = frequencies.shape[1]
    traits = phenotypes.shape[1]
    groups = lax.axis_size("animal")
    animals_all = float(groups * rows)
    quarter = rows // 4
    small = pltpu.CompilerParams(vmem_limit_bytes=12 * 2**20)
    genotypes = pltpu.with_memory_space_constraint(genotypes, pltpu.HBM)
    frequencies = pltpu.with_memory_space_constraint(frequencies, pltpu.HBM)

    blocks = [(True, True, quarter, 0, quarter), (True, False, quarter, 0, quarter), (False, True, quarter, 0, quarter), (False, False, quarter, 0, quarter)]
    to_core, panel, ahead = projection(blocks, AHEAD, 0, genotypes, frequencies, None)
    received = lax.ppermute(to_core, "marker", OTHER_CORE)
    kept, panel, ahead = projection(blocks, AHEAD, 1, genotypes, panel, ahead, (to_core,))
    to_chip = kept + received
    from_chip = lax.ppermute(to_chip, "marker", OTHER_CHIP)
    to_core, panel, ahead = projection(blocks, AHEAD, 2, genotypes, panel, ahead, (to_chip,))
    from_core = lax.ppermute(to_core, "marker", OTHER_CORE)
    kept, panel, ahead = projection(blocks, AHEAD, 3, genotypes, panel, ahead, (to_core,))
    with jax.named_scope("features"):
        features = pl.pallas_call(
            features_kernel,
            out_shape=jax.ShapeDtypeStruct((quarter, feats), jnp.bfloat16),
            in_specs=[vmem()] * 3,
            out_specs=vmem(),
            compiler_params=small,
        )(kept + from_chip, from_core, phases.reshape(1, feats))
    features_other = lax.ppermute(features, "marker", OTHER_CORE)

    height = feats // groups
    piece = (2 * height + height // 2, LANES)

    def gram_of(from_other_core, out_shape, *operands):
        return pl.pallas_call(
            functools.partial(gram_kernel, from_other_core),
            out_shape=out_shape,
            in_specs=[vmem()] * len(operands),
            out_specs=vmem(),
            compiler_params=small,
            cost_estimate=pl.CostEstimate(flops=feats * quarter * (feats + 2 * LANES), bytes_accessed=0, transcendentals=0),
        )(*operands)

    with jax.named_scope("gram_cross"):
        twice = jnp.concatenate([phenotypes, phenotypes], axis=1)
        partial_sums = gram_of(False, jax.ShapeDtypeStruct((feats, feats // 2 + LANES), jnp.float32), features, twice)
        partial_sums = gram_of(
            True, jax.ShapeDtypeStruct((groups,) + piece, jnp.bfloat16), features_other, twice, partial_sums
        )
    pieces = lax.all_to_all(partial_sums, "animal", 0, 0)
    with jax.named_scope("sum_animals"):
        own = pl.pallas_call(
            sum_kernel,
            out_shape=jax.ShapeDtypeStruct(piece, jnp.float32),
            in_specs=[vmem()],
            out_specs=vmem(),
            compiler_params=small,
        )(pieces)
    other = lax.ppermute(own, "marker", OTHER_CORE)
    with jax.named_scope("join_cores"):
        here = pl.pallas_call(
            join_kernel,
            out_shape=jax.ShapeDtypeStruct((own.shape[0] + 2 * height, LANES), jnp.float32),
            in_specs=[vmem()] * 2,
            out_specs=vmem(),
            compiler_params=small,
        )(own, other)
    there = lax.ppermute(here, "marker", OTHER_CHIP)
    with jax.named_scope("finish"):
        return pl.pallas_call(
            functools.partial(finish_kernel, animals_all),
            out_shape=(
                jax.ShapeDtypeStruct((feats // groups, feats), jnp.float32),
                jax.ShapeDtypeStruct((feats // groups, traits), jnp.float32),
            ),
            in_specs=[vmem()] * 2,
            out_specs=(vmem(), vmem()),
            compiler_params=small,
        )(here, there)


def solution(mesh):
    in_specs = (P("animal", "marker"), P("marker", None), P(), P("animal", None))
    out_specs = (P("animal", None), P("animal", None))
    return jax.shard_map(
        on_device, mesh=mesh, in_specs=in_specs, out_specs=out_specs, check_vma=False
    )
```
